256 devices in a mesh: section: 16 (over z, core), tp: 8 (over y, x_lo), dp: 2 (over x_hi).
Axes of the slice: x: 4 (x_hi: 2, x_lo: 2; x = x_hi * 2 + x_lo), y: 4, z: 8, core: 2. Of those that a mesh axis runs over, the one named last changes fastest.
Arguments:
- tokens: bfloat16 [1024, 8192], P('dp', 'tp'), parts along dimension 0, may hold values from -8 to 8
- ln_gain: float32 [16, 8192], P('section', 'tp'), may hold values from 0.5 to 1.5
- ln_bias: float32 [16, 8192], P('section', 'tp'), may hold values from -1.5 to 1.5
- w_qkv: bfloat16 [16, 8, 8192, 384], P('section', None, 'tp'), may hold values from -1 to 1
- w_out: bfloat16 [16, 1024, 8192], P('section', None, 'tp'), may hold values from -0.0625 to 0.0625
Outputs:
- states: bfloat16 [16, 1024, 8192], P('section', 'dp', 'tp'), parts along dimension 1
The draws below stay inside these ranges and needn't reach their ends.
There are 2 independent parts, one for each index of `dp`. The reference program is written for one: setup_inputs(seed, part) draws one part's arguments, and reference() takes and returns one part's arrays. A program takes and returns all parts, laid end to end along the dimension named above; an argument that names none is the same for every part. Nothing has to cross between parts.
All inputs are finite; a program needn't handle non-finite values.
Results may differ from the reference program's by a relative error of at most 0.03.
Values may be sent and summed in bfloat16 or wider, within the bound.
No kernel may reach another device: no remote copies, remote signals or barrier semaphores. Data moves between devices by JAX's collectives and lax.ppermute only.
A program may use at most 64 MiB of HBM per device.

```python
import math
import jax
import jax.numpy as jnp
from jax import lax

D = 8192
HD = 128
SPAN = 8
HEADS = 8
SEQ = 512
SECTIONS = 16
N_TP = 8


def draw_tokens(key, part):
    key = jax.random.fold_in(key, 5)
    noise_key, row_key = jax.random.split(key)
    position = jnp.arange(D, dtype=jnp.float32) / (D - 1)
    row_scale = jnp.exp(jax.random.uniform(row_key, (SEQ, 1), jnp.float32, -2.5, 0.5))
    noise = jax.random.normal(noise_key, (SEQ, D), jnp.float32)
    scale = 0.5 * jnp.exp(position * math.log(6.0))
    entries = noise * scale[None, :] * row_scale
    entries = jnp.clip(entries, -8.0, 8.0)
    return entries.astype(jnp.bfloat16)


def draw_w_qkv(key, part):
    key = jax.random.fold_in(key, 11)
    first_key = jax.random.fold_in(key, 0)
    entries = jax.random.normal(first_key, (SECTIONS, HEADS, D, 3 * HD), jnp.float32) * D ** (-0.5)
    entries = jnp.clip(entries, -1.0, 1.0)
    return entries.astype(jnp.bfloat16)


def draw_w_out(key, part):
    key = jax.random.fold_in(key, 17)
    first_key, second_key = jax.random.split(key)
    entries = jax.random.normal(first_key, (SECTIONS, HEADS * HD, N_TP, D // N_TP), jnp.float32)
    entries = entries * (SPAN * HEADS * HD) ** (-0.5)
    levels = jnp.exp(jax.random.uniform(second_key, (SECTIONS, 1, N_TP, 1), jnp.float32, -1.5, 1.0))
    entries = jnp.clip(entries * levels, -0.0625, 0.0625)
    return entries.reshape(SECTIONS, HEADS * HD, D).astype(jnp.bfloat16)


def shard_levels(rng, extent, cuts, low, largest):
    factor_of, own = 1.0, jax.random.fold_in(rng, 6)
    for dim, parts in cuts:
        steps = jnp.exp(jax.random.uniform(jax.random.fold_in(own, dim), (parts,), jnp.float32, low / len(cuts), largest / len(cuts)))
        factor_of = factor_of * jnp.repeat(steps, extent[dim] // parts).reshape([-1 if axis == dim else 1 for axis in range(len(extent))])
    return factor_of


def scatter_about(own_key, dims, deviation, limit, cuts=(), kind=jnp.bfloat16):
    result = deviation * jax.random.normal(own_key, dims, jnp.float32)
    if cuts:
        result = result * shard_levels(own_key, dims, cuts, -0.22, 0.18)
    return jnp.clip(result, -limit, limit).astype(kind)


def setup_inputs(seed: int = 0, part: int = 0) -> dict:
    arg_keys = jax.random.split(jax.random.key(seed), 6)
    part_splits = jax.random.split(jax.random.fold_in(arg_keys[5], part), 6)
    tokens = draw_tokens(jax.random.fold_in(jax.random.fold_in(arg_keys[5], part), 71), part)
    ln_gain = jnp.clip(1.0 + 0.1 * jax.random.normal(arg_keys[1], (SECTIONS, D), jnp.float32), 0.5, 1.5)
    ln_bias = scatter_about(arg_keys[2], (SECTIONS, D), 0.3, 1.5, ((0, 16), (1, 8)), jnp.float32)
    w_qkv = draw_w_qkv(jax.random.fold_in(arg_keys[5], 71), part)
    w_out = draw_w_out(jax.random.fold_in(arg_keys[5], 71), part)
    return {"tokens": tokens, "ln_gain": ln_gain, "ln_bias": ln_bias, "w_qkv": w_qkv, "w_out": w_out}


def reference(tokens, ln_gain, ln_bias, w_qkv, w_out):
    running = tokens
    layers = []
    positions = jnp.arange(SEQ)
    causal = positions[:, None] >= positions[None, :]
    columns = D // N_TP
    normed = None
    for number in range(SECTIONS):
        if number % SPAN == 0:
            first = number
            base_float = running.astype(jnp.float32)
            average = lax.optimization_barrier(jnp.sum(base_float, axis=1, keepdims=True)) / D
            variance = lax.optimization_barrier(jnp.sum(base_float * base_float, axis=1, keepdims=True)) / D - average * average
            normed = ((base_float - average) * lax.rsqrt(variance + 1e-05) * ln_gain[first].astype(jnp.float32) + ln_bias[first].astype(jnp.float32)).astype(jnp.bfloat16)
        joined = jnp.zeros((HEADS, SEQ, 3 * HD), jnp.float32)
        for block_num in range(N_TP):
            portion = jnp.einsum('rd,hdf->hrf', normed[:, block_num * columns:(block_num + 1) * columns].astype(jnp.float32), w_qkv[number][:, block_num * columns:(block_num + 1) * columns, :].astype(jnp.float32))
            joined = joined + lax.optimization_barrier(portion.astype(jnp.bfloat16)).astype(jnp.float32)
        joined = joined.astype(jnp.bfloat16)
        query = joined[:, :, :HD].astype(jnp.float32)
        keyed = joined[:, :, HD:2 * HD].astype(jnp.float32)
        valued = joined[:, :, 2 * HD:].astype(jnp.float32)
        scores = jnp.einsum('hqd,hkd->hqk', query, keyed) / jnp.sqrt(jnp.float32(HD))
        scores = jnp.where(causal[None, :, :], scores, -1e+30)
        highest = lax.optimization_barrier(jnp.max(scores, axis=-1, keepdims=True))
        lifted = jnp.exp(scores - highest)
        weights = (lifted / lax.optimization_barrier(jnp.sum(lifted, axis=-1, keepdims=True))).astype(jnp.bfloat16)
        attended = jnp.einsum('hqk,hkd->hqd', weights.astype(jnp.float32), valued).astype(jnp.bfloat16)
        flattened = jnp.transpose(attended, (1, 0, 2)).reshape(SEQ, HEADS * HD)
        projected = jnp.dot(flattened, w_out[number], preferred_element_type=jnp.float32)
        running = (running.astype(jnp.float32) + projected).astype(jnp.bfloat16)
        layers.append(running)
    return jnp.stack(layers)
```

```python
import functools

import jax
import jax.numpy as jnp
from jax import lax
from jax.experimental import pallas as pl
from jax.experimental.pallas import tpu as pltpu
from jax.sharding import PartitionSpec as P

SPAN = 8
TP = 8
CHIPS = 4
EXTRA = 16
SEGMENT = 256
EPS = 1e-05
BLOCKS = 1
BF16 = jnp.bfloat16
F32 = jnp.float32
VMEM = pl.BlockSpec(memory_space=pltpu.VMEM)
SMEM = pl.BlockSpec(memory_space=pltpu.SMEM)
HBM = pl.BlockSpec(memory_space=pl.ANY)


def params(mib):
    return pltpu.CompilerParams(vmem_limit_bytes=mib * 1024 * 1024)


def split_parts(value, count):
    parts = []
    for _ in range(count):
        part = value.astype(BF16).astype(F32)
        parts.append(part)
        value = value - part
    return parts


def segments_of(rows, limit=SEGMENT):
    size = min(rows, limit, SEGMENT)
    return [(start, size) for start in range(0, rows, size)]


def qkv_kernel(blocks, piece_count, *refs):
    refs = list(refs)
    place = refs.pop(0)
    x_ref = refs.pop(0)
    own_pieces = [refs.pop(0) for _ in range(piece_count)]
    other_pieces = [refs.pop(0) for _ in range(piece_count)]
    gain_ref, bias_ref, w_ref = refs.pop(0), refs.pop(0), refs.pop(0)
    base_ref = refs.pop(0) if piece_count else None
    outs = [[refs.pop(0) for _ in range(TP)] for _ in range(blocks)]
    lhs, w_buf, sems = refs
    me, core, chip, layer = place[0], place[1], place[2], place[3]
    rows, columns = x_ref.shape
    part_rows = rows // blocks

    copies = []
    for d in range(TP):
        copy = pltpu.make_async_copy(w_ref.at[jnp.bitwise_xor(me, d)], w_buf.at[d], sems.at[d])
        copy.start()
        copies.append(copy)

    if piece_count:
        base_ref[...] = x_ref[...]
        size = rows // (2 * CHIPS)

        @pl.when(layer == 1)
        def _():
            for half, pieces in ((core, own_pieces), (1 - core, other_pieces)):
                for d in range(CHIPS):
                    start = half * (rows // 2) + jnp.bitwise_xor(chip, d) * size
                    place_rows = pl.ds(pl.multiple_of(start, size), size)
                    base_ref[place_rows, :] = (
                        x_ref[place_rows, :].astype(F32) + pieces[d][...].astype(F32)
                    ).astype(BF16)

        source = base_ref
    else:
        source = x_ref

    gain = gain_ref[...]
    bias = bias_ref[...]
    stats = []
    for start, size in segments_of(rows, part_rows):
        value = source[start : start + size, :].astype(F32)
        first = jnp.sum(value, axis=1, keepdims=True)
        second = jnp.sum(value * value, axis=1, keepdims=True)
        centred = (value - first * (1.0 / columns)) * gain
        lhs[start : start + size, :] = centred.astype(BF16)
        lane = lax.broadcasted_iota(jnp.int32, (size, 128), 1)
        table = jnp.where(lane == 0, first, jnp.where(lane == 1, second, 0.0))
        stats.append(table.T[0:8, :])
    row16 = lax.broadcasted_iota(jnp.int32, (EXTRA, columns), 0)
    vectors = split_parts(gain, 2) + split_parts(bias, 2)
    tail = jnp.zeros((EXTRA, columns), F32)
    for number, vector in enumerate(vectors):
        tail = tail + jnp.where(row16 == number, vector, 0.0)
    lhs[rows : rows + EXTRA, :] = tail.astype(BF16)

    width = w_buf.shape[2]
    per_block = len(stats) // blocks
    out_row = lax.broadcasted_iota(jnp.int32, (EXTRA, width), 0)
    stat_tables = []
    for block in range(blocks):
        table = jnp.zeros((EXTRA, width), F32)
        for kind in range(2):
            for segment in range(per_block):
                line = stats[block * per_block + segment][kind : kind + 1, :]
                for number, part in enumerate(split_parts(line, 3)):
                    padded = jnp.concatenate(
                        [part, jnp.zeros((1, width - part.shape[1]), F32)], axis=1
                    )
                    slot = 4 + (kind * per_block + segment) * 3 + number
                    table = table + jnp.where(out_row == slot, padded, 0.0)
        stat_tables.append(table)

    for d in range(TP):
        copies[d].wait()
        result = jnp.dot(lhs[...], w_buf[d], preferred_element_type=F32)
        ends = result[rows : rows + EXTRA, :]
        summed = split_parts(ends[0:1] + ends[1:2], 2) + split_parts(ends[2:3] + ends[3:4], 2)
        head_table = jnp.zeros((EXTRA, width), F32)
        for number, vector in enumerate(summed):
            head_table = head_table + jnp.where(out_row == number, vector, 0.0)
        for block in range(blocks):
            start = block * part_rows
            outs[block][d][0:part_rows, :] = result[start : start + part_rows, :].astype(BF16)
            outs[block][d][part_rows : part_rows + EXTRA, :] = (
                head_table + stat_tables[block]
            ).astype(BF16)


def qkv(place, x, pieces, others, gain, bias, w, blocks):
    rows, columns = x.shape
    heads, _, width = w.shape
    piece_count = len(pieces)
    shapes = [jax.ShapeDtypeStruct((rows // blocks + EXTRA, width), BF16)] * (TP * blocks)
    if piece_count:
        shapes = [jax.ShapeDtypeStruct((rows, columns), BF16)] + shapes
    out = pl.pallas_call(
        functools.partial(qkv_kernel, blocks, piece_count),
        out_shape=shapes,
        in_specs=[SMEM, VMEM] + [VMEM] * (2 * piece_count) + [VMEM, VMEM, HBM],
        out_specs=[VMEM] * len(shapes),
        scratch_shapes=[
            pltpu.VMEM((rows + EXTRA, columns), BF16),
            pltpu.VMEM((heads, columns, width), BF16),
            pltpu.SemaphoreType.DMA((TP,)),
        ],
        compiler_params=params(32),
        cost_estimate=pl.CostEstimate(
            flops=2 * rows * columns * heads * width,
            bytes_accessed=2 * heads * columns * width,
            transcendentals=0,
        ),
        name="qkv",
    )(place, x, *pieces, *others, gain, bias, w)
    out = list(out)
    base = out.pop(0) if piece_count else x
    return base, [out[block * TP : (block + 1) * TP] for block in range(blocks)]


def attention_kernel(previous, total_features, *refs):
    refs = list(refs)
    pieces = [refs.pop(0) for _ in range(TP)]
    old_keys = [refs.pop(0) for _ in range(previous)]
    old_values = [refs.pop(0) for _ in range(previous)]
    out_ref, key_ref, value_ref = refs
    rows = out_ref.shape[0]
    head_dim = out_ref.shape[1]
    width = 3 * head_dim
    segments = segments_of(rows)

    total = jnp.zeros((rows, width), F32)
    first_lines, second_lines, head_lines = [], [], []
    offset = jnp.zeros((1, width), F32)
    for piece in pieces:
        total = total + piece[0:rows, :].astype(F32)
        ends = piece[rows : rows + EXTRA, :].astype(F32)
        head_lines.append(ends[0:1] + ends[1:2])
        offset = offset + (ends[2:3] + ends[3:4])
        lines = []
        for kind in range(2):
            spans = []
            for segment, (_, size) in enumerate(segments):
                slot = 4 + (kind * len(segments) + segment) * 3
                spans.append((ends[slot : slot + 1] + ends[slot + 1 : slot + 2] + ends[slot + 2 : slot + 3])[:, :size])
            lines.append(jnp.concatenate(spans, axis=1) if len(spans) > 1 else spans[0])
        first_lines.append(lines[0])
        second_lines.append(lines[1])
    average = sum(first_lines) * (1.0 / total_features)
    variance = sum(second_lines) * (1.0 / total_features) - average * average
    scale = lax.rsqrt(variance + EPS)
    line_row = lax.broadcasted_iota(jnp.int32, (128, rows), 0)
    table = jnp.where(line_row == TP, scale, 0.0)
    head_row = lax.broadcasted_iota(jnp.int32, (128, width), 0)
    heads = jnp.zeros((128, width), F32)
    for d in range(TP):
        table = jnp.where(line_row == d, first_lines[d] * (TP / total_features) - average, table)
        heads = jnp.where(head_row == d, head_lines[d], heads)
    turned = table.T
    shift = jnp.dot(turned, heads, preferred_element_type=F32, precision=lax.Precision.HIGHEST)
    joined = ((total + shift) * turned[:, TP : TP + 1] + offset).astype(BF16)
    query = joined[:, :head_dim]
    key = joined[:, head_dim : 2 * head_dim]
    value = joined[:, 2 * head_dim :]
    key_ref[...] = key
    value_ref[...] = value
    keys = jnp.concatenate([old[...] for old in old_keys] + [key], axis=0) if previous else key
    values = jnp.concatenate([old[...] for old in old_values] + [value], axis=0) if previous else value
    length = (previous + 1) * rows
    scores = lax.dot_general(
        query, keys, (((1,), (1,)), ((), ())), preferred_element_type=F32
    ) * (1.0 / head_dim**0.5)
    at_query = lax.broadcasted_iota(jnp.int32, (rows, length), 0) + previous * rows
    at_key = lax.broadcasted_iota(jnp.int32, (rows, length), 1)
    scores = jnp.where(at_key <= at_query, scores, -1e30)
    highest = jnp.max(scores, axis=1, keepdims=True)
    lifted = jnp.exp(scores - highest)
    weights = (lifted * (1.0 / jnp.sum(lifted, axis=1, keepdims=True))).astype(BF16)
    out_ref[...] = jnp.dot(weights, values, preferred_element_type=F32).astype(BF16)


def attention(pieces, old, total_features):
    rows = pieces[0].shape[0] - EXTRA
    head_dim = pieces[0].shape[1] // 3
    shape = jax.ShapeDtypeStruct((rows, head_dim), BF16)
    length = (len(old) + 1) * rows
    return pl.pallas_call(
        functools.partial(attention_kernel, len(old), total_features),
        out_shape=[shape] * 3,
        in_specs=[VMEM] * (TP + 2 * len(old)),
        out_specs=[VMEM] * 3,
        compiler_params=params(24),
        cost_estimate=pl.CostEstimate(
            flops=4 * rows * length * head_dim, bytes_accessed=6 * TP * rows * head_dim, transcendentals=rows * length
        ),
        name="attention",
    )(*pieces, *[k for k, _ in old], *[v for _, v in old])


def project_kernel(passing, place, *refs):
    refs = list(refs)
    pieces = [refs.pop(0) for _ in range(TP)]
    w_ref = refs.pop(0)
    old = [refs.pop(0) for _ in range(2)] if passing else None
    keep_ref, send_ref, side = refs
    me, core, layer = place[0], place[1], place[3]
    rows, head_dim = pieces[0].shape

    def work():
        for d in range(TP):
            start = pl.multiple_of(jnp.bitwise_xor(me, d) * head_dim, head_dim)
            side[:, pl.ds(start, head_dim)] = pieces[d][...]
        for half, target in ((core, keep_ref), (1 - core, send_ref)):
            place_rows = pl.ds(pl.multiple_of(half * (rows // 2), rows // 2), rows // 2)
            target[...] = jnp.dot(
                side[place_rows, :], w_ref[...], preferred_element_type=F32
            ).astype(BF16)

    if passing:
        pl.when(layer == 1)(work)

        @pl.when(layer == 0)
        def _():
            keep_ref[...] = old[0][...]
            send_ref[...] = old[1][...]
    else:
        work()


def project(place, pieces, w, old):
    rows, head_dim = pieces[0].shape
    columns = w.shape[1]
    shape = jax.ShapeDtypeStruct((rows // 2, columns), BF16)
    old = list(old) if old else []
    return pl.pallas_call(
        functools.partial(project_kernel, bool(old)),
        out_shape=[shape] * 2,
        in_specs=[SMEM] + [VMEM] * (TP + 1 + len(old)),
        out_specs=[VMEM] * 2,
        scratch_shapes=[pltpu.VMEM((rows, TP * head_dim), BF16)],
        compiler_params=params(24),
        cost_estimate=pl.CostEstimate(
            flops=2 * rows * TP * head_dim * columns, bytes_accessed=2 * w.size + 2 * rows * columns, transcendentals=0
        ),
        name="project",
    )(place, *pieces, w, *old)


def quarters_kernel(place, keep_ref, got_ref, *outs):
    chip = place[2]
    size = outs[0].shape[0]
    for d in range(CHIPS):
        place_rows = pl.ds(pl.multiple_of(jnp.bitwise_xor(chip, d) * size, size), size)
        outs[d][...] = (
            keep_ref[place_rows, :].astype(F32) + got_ref[place_rows, :].astype(F32)
        ).astype(BF16)


def quarters(place, keep, got):
    rows, columns = keep.shape
    shape = jax.ShapeDtypeStruct((rows // CHIPS, columns), BF16)
    return pl.pallas_call(
        quarters_kernel,
        out_shape=[shape] * CHIPS,
        in_specs=[SMEM, VMEM, VMEM],
        out_specs=[VMEM] * CHIPS,
        compiler_params=params(16),
        name="quarters",
    )(place, keep, got)


def finish_kernel(place, base_ref, keep_ref, got_ref, send_ref, other_keep_ref, *refs):
    own, others, out_ref = refs[:CHIPS], refs[CHIPS : 2 * CHIPS], refs[2 * CHIPS]
    core, chip = place[1], place[2]
    half_rows = keep_ref.shape[0]
    size = half_rows // CHIPS
    second = core.astype(F32)
    for half, sums, mine, theirs in (
        (core, own, keep_ref, got_ref),
        (1 - core, others, send_ref, other_keep_ref),
    ):
        for d in range(CHIPS):
            start = pl.multiple_of(jnp.bitwise_xor(chip, d) * size, size)
            inside = pl.ds(start, size)
            whole = pl.ds(pl.multiple_of(half * half_rows + start, size), size)
            out_ref[whole, :] = (
                base_ref[whole, :].astype(F32)
                + sums[d][...].astype(F32)
                + mine[inside, :].astype(F32)
                + second * theirs[inside, :].astype(F32)
            ).astype(BF16)


def finish(place, base, keep, got, send, other_keep, own, others):
    return pl.pallas_call(
        finish_kernel,
        out_shape=jax.ShapeDtypeStruct(base.shape, BF16),
        in_specs=[SMEM] + [VMEM] * (5 + 2 * CHIPS),
        out_specs=VMEM,
        compiler_params=params(24),
        name="finish",
    )(place, base, keep, got, send, other_keep, *own, *others)


def over_tp(value, d):
    return lax.ppermute(value, "tp", [(t, t ^ d) for t in range(TP)])


def over_cores(value):
    return lax.ppermute(value, "section", [(s, s ^ 1) for s in range(2 * SPAN)])


def over_chips(value, d):
    return lax.ppermute(value, "section", [(s, s ^ (2 * d)) for s in range(2 * SPAN)])


def spread(value):
    return [value] + [over_tp(value, d) for d in range(1, TP)]


def scatter(pieces):
    return [pieces[0]] + [over_tp(pieces[d], d) for d in range(1, TP)]


def on_device(tokens, ln_gain, ln_bias, w_qkv, w_out):
    section = lax.axis_index("section")
    me = lax.axis_index("tp")
    core = section % 2
    chip = (section // 2) % CHIPS
    layer = section // SPAN
    place = jnp.stack([me, core, chip, layer]).astype(jnp.int32)
    weight_in = w_qkv[0]
    weight_back = w_out[0]
    features = tokens.shape[1] * TP
    rows = tokens.shape[0]
    part = rows // BLOCKS

    vectors = jnp.concatenate([ln_gain, ln_bias], axis=0)
    sent = [
        lax.ppermute(vectors, "section", [(g, g + 2 * d) for g in (0, SPAN)]) for d in range(1, CHIPS)
    ]
    even = jnp.where(chip == 0, vectors, sent[0] + sent[1] + sent[2])
    odd = lax.ppermute(even, "section", [(s, s + 1) for s in range(0, 2 * SPAN, 2)])
    vectors = jnp.where(core == 0, even, odd)
    gain, bias = vectors[0:1], vectors[1:2]

    _, parts = qkv(place, tokens, [], [], gain, bias, weight_in, BLOCKS)
    pieces = [scatter(parts[block]) for block in range(BLOCKS)]
    sums, kept, old = [], [], []
    for block in range(BLOCKS):
        out, key, value = attention(pieces[block], old, features)
        old.append((key, value))
        keep, send = project(place, spread(out), weight_back, None)
        kept.append((keep, send))
        got = over_cores(send)
        quarter = quarters(place, keep, got)
        arrived = [quarter[0]] + [over_chips(quarter[d], d) for d in range(1, CHIPS)]
        total = sum(value.astype(F32) for value in arrived).astype(BF16)
        total = lax.ppermute(total, "section", [(s, s + SPAN) for s in range(SPAN)])
        own = [total] + [over_chips(total, d) for d in range(1, CHIPS)]
        sums.append((own, [over_cores(value) for value in own]))

    outputs, old = [], []
    for block in range(BLOCKS):
        x = tokens[block * part : (block + 1) * part]
        base, parts = qkv(place, x, *sums[block], gain, bias, weight_in, 1)
        out, key, value = attention(scatter(parts[0]), old, features)
        old.append((key, value))
        keep, send = project(place, spread(out), weight_back, kept[block])
        got = over_cores(send)
        other_keep = over_cores(keep)
        quarter = quarters(place, keep, got)
        arrived = [quarter[0]] + [over_chips(quarter[d], d) for d in range(1, CHIPS)]
        before = []
        for d in range(CHIPS):
            target = jnp.bitwise_xor(chip, d)
            before.append(
                sum(
                    jnp.where(jnp.bitwise_xor(chip, e) < target, arrived[e].astype(F32), 0.0)
                    for e in range(CHIPS)
                ).astype(BF16)
            )
        own = [before[0]] + [over_chips(before[d], d) for d in range(1, CHIPS)]
        others = [over_cores(value) for value in own]
        outputs.append(finish(place, base, keep, got, send, other_keep, own, others))
    return (outputs[0] if BLOCKS == 1 else jnp.concatenate(outputs, axis=0))[None]


def solution(mesh):
    return jax.shard_map(
        on_device,
        mesh=mesh,
        in_specs=(
            P("dp", "tp"),
            P("section", "tp"),
            P("section", "tp"),
            P("section", None, "tp", None),
            P("section", None, "tp"),
        ),
        out_specs=P("section", "dp", "tp"),
        check_vma=False,
    )
```

```python
import functools

import jax
import jax.numpy as jnp
from jax import lax
from jax.experimental import pallas as pl
from jax.experimental.pallas import tpu as pltpu
from jax.sharding import PartitionSpec as P

SPAN = 8
TP = 8
CHIPS = 4
EXTRA = 16
EPS = 1e-05
SEGMENT = 256
BLOCKS = 1
BF16 = jnp.bfloat16
F32 = jnp.float32
VMEM = pl.BlockSpec(memory_space=pltpu.VMEM)
SMEM = pl.BlockSpec(memory_space=pltpu.SMEM)
HBM = pl.BlockSpec(memory_space=pl.ANY)


def params(mib):
    return pltpu.CompilerParams(vmem_limit_bytes=mib * 1024 * 1024)


def segments_of(rows):
    size = min(rows, SEGMENT)
    return [(start, size) for start in range(0, rows, size)]


def split_parts(value, count):
    parts = []
    for _ in range(count):
        part = value.astype(BF16).astype(F32)
        parts.append(part)
        value = value - part
    return parts


def ending(head_line, offset_line, first, second, width):
    vectors = split_parts(head_line, 2) + split_parts(offset_line, 2)
    for line in (first, second):
        for start, size in segments_of(line.shape[1]):
            for part in split_parts(line[:, start : start + size], 3):
                vectors.append(jnp.concatenate([part, jnp.zeros((1, width - size), F32)], axis=1))
    row = lax.broadcasted_iota(jnp.int32, (EXTRA, width), 0)
    table = jnp.zeros((EXTRA, width), F32)
    for number, vector in enumerate(vectors):
        table = table + jnp.where(row == number, vector, 0.0)
    return table


def combine(pieces, features):
    rows, width = pieces[0].shape[0] - EXTRA, pieces[0].shape[1]
    segments = segments_of(rows)
    total = jnp.zeros((rows, width), F32)
    heads, firsts, offset, second = [], [], 0.0, 0.0
    for piece in pieces:
        total = total + piece[0:rows, :].astype(F32)
        ends = piece[rows : rows + EXTRA, :].astype(F32)
        heads.append(ends[0:1] + ends[1:2])
        offset = offset + (ends[2:3] + ends[3:4])
        lines = []
        for kind in range(2):
            spans = []
            for number, (_, size) in enumerate(segments):
                slot = 4 + (kind * len(segments) + number) * 3
                spans.append((ends[slot : slot + 1] + ends[slot + 1 : slot + 2] + ends[slot + 2 : slot + 3])[:, :size])
            lines.append(jnp.concatenate(spans, axis=1) if len(spans) > 1 else spans[0])
        firsts.append(lines[0])
        second = second + lines[1]
    first = sum(firsts)
    count = features * len(pieces)
    average = first * (1.0 / count)
    variance = second * (1.0 / count) - average * average
    scale = lax.rsqrt(jnp.maximum(variance, 0.0) + EPS)
    line_row = lax.broadcasted_iota(jnp.int32, (128, rows), 0)
    table = jnp.where(line_row == TP, scale, 0.0)
    head_row = lax.broadcasted_iota(jnp.int32, (128, width), 0)
    matrix = jnp.zeros((128, width), F32)
    for number in range(len(pieces)):
        table = jnp.where(line_row == number, firsts[number] * (1.0 / features) - average, table)
        matrix = jnp.where(head_row == number, heads[number], matrix)
    turned = table.T
    total = total + jnp.dot(
        turned, matrix, preferred_element_type=F32, precision=lax.Precision.HIGHEST
    )
    return total, turned[:, TP : TP + 1], offset


def cheap():
    return pl.CostEstimate(flops=1, bytes_accessed=1, transcendentals=0)


def qkv_kernel(block, layered, after_count, *refs):
    refs = list(refs)
    place, x_ref = refs.pop(0), refs.pop(0)
    pieces = [refs.pop(0) for _ in range(2)] if layered else []
    gain_ref, bias_ref, w_ref = refs.pop(0), refs.pop(0), refs.pop(0)
    del refs[:after_count]
    base_ref = refs.pop(0) if layered else None
    out_ref, lhs, w_buf, sems = refs
    core, layer = place[1], place[3]
    columns = x_ref.shape[1]
    rows = lhs.shape[0] - EXTRA
    width = w_buf.shape[2]

    copies = []
    for head in range(TP):
        copy = pltpu.make_async_copy(w_ref.at[head], w_buf.at[head], sems.at[head])
        copy.start()
        copies.append(copy)

    if layered:
        half_rows = rows // 2
        for half, piece in ((core, pieces[0]), (1 - core, pieces[1])):
            target = pl.ds(pl.multiple_of(half * half_rows, half_rows), half_rows)
            tokens = x_ref[target, :].astype(F32)
            added = tokens + piece[...].astype(F32)
            base_ref[target, :] = jnp.where(layer == 1, added, tokens).astype(BF16)
        source = base_ref
    else:
        source = x_ref

    gain = gain_ref[...]
    bias = bias_ref[...]
    value = source[...].astype(F32)
    first = jnp.sum(value, axis=1, keepdims=True)
    second = jnp.sum(value * value, axis=1, keepdims=True)
    lhs[0:rows, :] = ((value - first * (1.0 / columns)) * gain).astype(BF16)
    lane = lax.broadcasted_iota(jnp.int32, (rows, 128), 1)
    turned = jnp.where(lane == 0, first, jnp.where(lane == 1, second, 0.0)).T
    row16 = lax.broadcasted_iota(jnp.int32, (EXTRA, columns), 0)
    tail = jnp.zeros((EXTRA, columns), F32)
    for number, vector in enumerate(split_parts(gain, 2) + split_parts(bias, 2)):
        tail = tail + jnp.where(row16 == number, vector, 0.0)
    lhs[rows : rows + EXTRA, :] = tail.astype(BF16)
    blank = jnp.zeros((1, width), F32)
    lines = ending(blank, blank, turned[0:1, :], turned[1:2, :], width)
    out_row = lax.broadcasted_iota(jnp.int32, (EXTRA, width), 0)

    for head in range(TP):
        copies[head].wait()
        result = jnp.dot(lhs[...], w_buf[head], preferred_element_type=F32)
        ends = result[rows : rows + EXTRA, :]
        table = lines
        vectors = split_parts(ends[0:1] + ends[1:2], 2) + split_parts(ends[2:3] + ends[3:4], 2)
        for number, vector in enumerate(vectors):
            table = table + jnp.where(out_row == number, vector, 0.0)
        out_ref[head, 0:rows, :] = result[0:rows, :].astype(BF16)
        out_ref[head, rows : rows + EXTRA, :] = table.astype(BF16)


def whole(shape):
    return pl.BlockSpec(shape, lambda _: (0,) * len(shape))


def qkv(place, x, block, pieces, gain, bias, w, after):
    rows, columns = x.shape[0] // BLOCKS, x.shape[1]
    heads, _, width = w.shape
    shapes = [jax.ShapeDtypeStruct((heads, rows + EXTRA, width), BF16)]
    if pieces:
        shapes = [jax.ShapeDtypeStruct((rows, columns), BF16)] + shapes
    out = pl.pallas_call(
        functools.partial(qkv_kernel, block, bool(pieces), len(after)),
        grid=(1,),
        out_shape=shapes,
        in_specs=[SMEM, pl.BlockSpec((rows, columns), lambda _: (block, 0))]
        + [whole(value.shape) for value in pieces]
        + [whole(gain.shape), whole(bias.shape), HBM]
        + [HBM] * len(after),
        out_specs=[whole(shape.shape) for shape in shapes],
        scratch_shapes=[
            pltpu.VMEM((rows + EXTRA, columns), BF16),
            pltpu.VMEM((heads, columns, width), BF16),
            pltpu.SemaphoreType.DMA((TP,)),
        ],
        compiler_params=params(48),
        cost_estimate=cheap(),
        name="qkv",
    )(place, x, *pieces, gain, bias, w, *after)
    return out if pieces else (None, out[0])


def attention_kernel(previous, features, after_count, *refs):
    refs = list(refs)
    pieces_ref = refs.pop(0)
    old_keys = [refs.pop(0) for _ in range(previous)]
    old_values = [refs.pop(0) for _ in range(previous)]
    del refs[:after_count]
    out_ref, key_ref, value_ref = refs
    rows, head_dim = out_ref.shape
    total, scale, offset = combine([pieces_ref.at[t] for t in range(TP)], features // TP)
    joined = (total * scale + offset).astype(BF16)
    query = joined[:, :head_dim]
    key = joined[:, head_dim : 2 * head_dim]
    value = joined[:, 2 * head_dim :]
    key_ref[...] = key
    value_ref[...] = value
    keys = jnp.concatenate([old[...] for old in old_keys] + [key], axis=0) if previous else key
    values = jnp.concatenate([old[...] for old in old_values] + [value], axis=0) if previous else value
    length = (previous + 1) * rows
    scores = lax.dot_general(
        query, keys, (((1,), (1,)), ((), ())), preferred_element_type=F32
    ) * (1.0 / head_dim**0.5)
    at_query = lax.broadcasted_iota(jnp.int32, (rows, length), 0) + previous * rows
    at_key = lax.broadcasted_iota(jnp.int32, (rows, length), 1)
    scores = jnp.where(at_key <= at_query, scores, -1e30)
    highest = jnp.max(scores, axis=1, keepdims=True)
    lifted = jnp.exp(scores - highest)
    weights = (lifted * (1.0 / jnp.sum(lifted, axis=1, keepdims=True))).astype(BF16)
    out_ref[...] = jnp.dot(weights, values, preferred_element_type=F32).astype(BF16)


def attention(pieces, old, features, after):
    rows = pieces.shape[1] - EXTRA
    head_dim = pieces.shape[2] // 3
    shape = jax.ShapeDtypeStruct((rows, head_dim), BF16)
    return pl.pallas_call(
        functools.partial(attention_kernel, len(old), features, len(after)),
        out_shape=[shape] * 3,
        in_specs=[VMEM] * (1 + 2 * len(old)) + [HBM] * len(after),
        out_specs=[VMEM] * 3,
        compiler_params=params(24),
        cost_estimate=cheap(),
        name="attention",
    )(pieces, *[k for k, _ in old], *[v for _, v in old], *after)


def project_kernel(passing, after_count, place, *refs):
    refs = list(refs)
    pieces = [refs.pop(0) for _ in range(TP)]
    w_ref = refs.pop(0)
    old = [refs.pop(0) for _ in range(2)] if passing else None
    del refs[:after_count]
    keep_ref, send_ref, side = refs
    me, core, layer = place[0], place[1], place[3]
    rows, head_dim = pieces[0].shape

    def work():
        for d in range(TP):
            start = pl.multiple_of(jnp.bitwise_xor(me, d) * head_dim, head_dim)
            side[:, pl.ds(start, head_dim)] = pieces[d][...]
        for half, target in ((1 - core, send_ref), (core, keep_ref)):
            place_rows = pl.ds(pl.multiple_of(half * (rows // 2), rows // 2), rows // 2)
            target[...] = jnp.dot(
                side[place_rows, :], w_ref[...], preferred_element_type=F32
            ).astype(BF16)

    if passing:
        pl.when(layer == 1)(work)

        @pl.when(layer == 0)
        def _():
            keep_ref[...] = old[0][...]
            send_ref[...] = old[1][...]
    else:
        work()


def project(place, pieces, w, old, after):
    rows, head_dim = pieces[0].shape
    columns = w.shape[1]
    shape = jax.ShapeDtypeStruct((rows // 2, columns), BF16)
    old = list(old) if old else []
    return pl.pallas_call(
        functools.partial(project_kernel, bool(old), len(after)),
        out_shape=[shape] * 2,
        in_specs=[SMEM] + [VMEM] * (TP + 1 + len(old)) + [HBM] * len(after),
        out_specs=[VMEM] * 2,
        scratch_shapes=[pltpu.VMEM((rows, TP * head_dim), BF16)],
        compiler_params=params(24),
        cost_estimate=cheap(),
        name="project",
    )(place, *pieces, w, *old, *after)


def quarters_kernel(place, keep_ref, got_ref, *outs):
    chip = place[2]
    size = outs[0].shape[0]
    for d in range(CHIPS):
        rows = pl.ds(pl.multiple_of(jnp.bitwise_xor(chip, d) * size, size), size)
        outs[d][...] = (keep_ref[rows, :].astype(F32) + got_ref[rows, :].astype(F32)).astype(BF16)


def quarters(place, keep, got):
    rows, columns = keep.shape
    return pl.pallas_call(
        quarters_kernel,
        out_shape=[jax.ShapeDtypeStruct((rows // CHIPS, columns), BF16)] * CHIPS,
        in_specs=[SMEM, VMEM, VMEM],
        out_specs=[VMEM] * CHIPS,
        compiler_params=params(16),
        cost_estimate=cheap(),
        name="quarters",
    )(place, keep, got)


def arrange_kernel(after_count, place, *refs):
    chip = place[2]
    out_ref = refs[CHIPS + after_count]
    size = out_ref.shape[0] // CHIPS
    for d in range(CHIPS):
        rows = pl.ds(pl.multiple_of(jnp.bitwise_xor(chip, d) * size, size), size)
        out_ref[rows, :] = refs[d][...]


def arrange(place, pieces, after):
    rows, columns = pieces[0].shape
    return pl.pallas_call(
        functools.partial(arrange_kernel, len(after)),
        out_shape=jax.ShapeDtypeStruct((rows * CHIPS, columns), BF16),
        in_specs=[SMEM] + [VMEM] * CHIPS + [HBM] * len(after),
        out_specs=VMEM,
        compiler_params=params(16),
        cost_estimate=cheap(),
        name="arrange",
    )(place, *pieces, *after)


def finish_kernel(place, base_ref, keep_ref, got_ref, send_ref, other_keep_ref, own_ref, other_ref, out_ref):
    core = place[1]
    half_rows = keep_ref.shape[0]
    second = core.astype(F32)
    for half, sums, mine, theirs in (
        (core, own_ref, keep_ref, got_ref),
        (1 - core, other_ref, send_ref, other_keep_ref),
    ):
        rows = pl.ds(pl.multiple_of(half * half_rows, half_rows), half_rows)
        out_ref[rows, :] = (
            base_ref[rows, :].astype(F32)
            + sums[...].astype(F32)
            + mine[...].astype(F32)
            + second * theirs[...].astype(F32)
        ).astype(BF16)


def finish(place, base, *values):
    return pl.pallas_call(
        finish_kernel,
        out_shape=jax.ShapeDtypeStruct(base.shape, BF16),
        in_specs=[SMEM] + [VMEM] * (1 + len(values)),
        out_specs=VMEM,
        compiler_params=params(24),
        cost_estimate=cheap(),
        name="finish",
    )(place, base, *values)


def over_tp(value):
    return lax.all_to_all(value, "tp", 0, 0, tiled=True)


def over_cores(value):
    return lax.ppermute(value, "section", [(s, s ^ 1) for s in range(2 * SPAN)])


def over_chips(value, d):
    return lax.ppermute(value, "section", [(s, s ^ (2 * d)) for s in range(2 * SPAN)])


def spread(value):
    return [value] + [
        lax.ppermute(value, "tp", [(t, t ^ d) for t in range(TP)]) for d in range(1, TP)
    ]


def over_layer(values):
    return [values[0]] + [over_chips(values[d], d) for d in range(1, CHIPS)]


def on_device(tokens, ln_gain, ln_bias, w_qkv, w_out):
    section = lax.axis_index("section")
    me = lax.axis_index("tp")
    core = section % 2
    chip = (section // 2) % CHIPS
    layer = section // SPAN
    place = jnp.stack([me, core, chip, layer]).astype(jnp.int32)
    weight_in = w_qkv[0]
    weight_back = w_out[0]
    features = tokens.shape[1] * TP

    vectors = jnp.concatenate([ln_gain, ln_bias], axis=0)
    even = vectors
    for d in range(1, CHIPS):
        even = jnp.where(chip == d, over_chips(vectors, d), even)
    vectors = jnp.where(core == 0, even, over_cores(even))
    gain, bias = vectors[0:1], vectors[1:2]

    steps = range(BLOCKS)
    pieces, kept, sums, totals = [], [], [], []
    after = []
    for block in steps:
        _, part = qkv(place, tokens, block, [], gain, bias, weight_in, after)
        pieces.append(over_tp(part))
        after = [part]
    old, after = [], []
    for block in steps:
        out, key, value = attention(pieces[block], old, features, after)
        old.append((key, value))
        keep, send = project(place, spread(out), weight_back, None, totals[-1:])
        kept.append((keep, send))
        quarter = quarters(place, keep, over_cores(send))
        after = [quarter[0]]
        total = sum(value.astype(F32) for value in over_layer(quarter)).astype(BF16)
        totals.append(total)
        half = arrange(place, [over_chips(total, CHIPS ^ d) for d in range(CHIPS)], [])
        sums.append((half, over_cores(half)))

    bases, pieces, old, after = [], [], [], totals[-1:]
    for block in steps:
        base, part = qkv(place, tokens, block, sums[block], gain, bias, weight_in, after)
        bases.append(base)
        pieces.append(over_tp(part))
        after = [part]
    outputs, gate = [], []
    for block in steps:
        out, key, value = attention(pieces[block], old, features, after)
        old.append((key, value))
        keep, send = project(place, spread(out), weight_back, kept[block], gate)
        got = over_cores(send)
        other_keep = over_cores(keep)
        quarter = quarters(place, keep, got)
        after = [quarter[0]]
        arrived = over_layer(quarter)
        before = []
        for d in range(CHIPS):
            target = jnp.bitwise_xor(chip, d)
            before.append(
                sum(
                    jnp.where(jnp.bitwise_xor(chip, e) < target, arrived[e].astype(F32), 0.0)
                    for e in range(CHIPS)
                ).astype(BF16)
            )
        gate = [before[0]]
        own = arrange(place, over_layer(before), [])
        outputs.append(finish(place, bases[block], keep, got, send, other_keep, own, over_cores(own)))
    return (outputs[0] if BLOCKS == 1 else jnp.concatenate(outputs, axis=0))[None]


def solution(mesh):
    return jax.shard_map(
        on_device,
        mesh=mesh,
        in_specs=(
            P("dp", "tp"),
            P("section", "tp"),
            P("section", "tp"),
            P("section", None, "tp", None),
            P("section", None, "tp"),
        ),
        out_specs=P("section", "dp", "tp"),
        check_vma=False,
    )
```

```python
import functools

import jax
import jax.numpy as jnp
from jax import lax
from jax.experimental import pallas as pl
from jax.experimental.pallas import tpu as pltpu
from jax.sharding import PartitionSpec as P

SPAN = 8
TP = 8
CHIPS = 4
EXTRA = 16
EPS = 1e-05
SEGMENT = 256
BF16 = jnp.bfloat16
F32 = jnp.float32
VMEM = pl.BlockSpec(memory_space=pltpu.VMEM)
SMEM = pl.BlockSpec(memory_space=pltpu.SMEM)
HBM = pl.BlockSpec(memory_space=pl.ANY)


def params(mib):
    return pltpu.CompilerParams(vmem_limit_bytes=mib * 1024 * 1024)


def segments_of(rows):
    size = min(rows, SEGMENT)
    return [(start, size) for start in range(0, rows, size)]


def split_parts(value, count):
    parts = []
    for _ in range(count):
        part = value.astype(BF16).astype(F32)
        parts.append(part)
        value = value - part
    return parts


def ending(head_line, offset_line, first, second, width):
    vectors = split_parts(head_line, 2) + split_parts(offset_line, 2)
    for line in (first, second):
        for start, size in segments_of(line.shape[1]):
            for part in split_parts(line[:, start : start + size], 3):
                vectors.append(jnp.concatenate([part, jnp.zeros((1, width - size), F32)], axis=1))
    row = lax.broadcasted_iota(jnp.int32, (EXTRA, width), 0)
    table = jnp.zeros((EXTRA, width), F32)
    for number, vector in enumerate(vectors):
        table = table + jnp.where(row == number, vector, 0.0)
    return table


def combine(pieces, features):
    rows, width = pieces[0].shape[0] - EXTRA, pieces[0].shape[1]
    segments = segments_of(rows)
    total = jnp.zeros((rows, width), F32)
    heads, firsts, offset, second = [], [], 0.0, 0.0
    for piece in pieces:
        total = total + piece[0:rows, :].astype(F32)
        ends = piece[rows : rows + EXTRA, :].astype(F32)
        heads.append(ends[0:1] + ends[1:2])
        offset = offset + (ends[2:3] + ends[3:4])
        lines = []
        for kind in range(2):
            spans = []
            for number, (_, size) in enumerate(segments):
                slot = 4 + (kind * len(segments) + number) * 3
                spans.append((ends[slot : slot + 1] + ends[slot + 1 : slot + 2] + ends[slot + 2 : slot + 3])[:, :size])
            lines.append(jnp.concatenate(spans, axis=1) if len(spans) > 1 else spans[0])
        firsts.append(lines[0])
        second = second + lines[1]
    first = sum(firsts)
    count = features * len(pieces)
    average = first * (1.0 / count)
    variance = second * (1.0 / count) - average * average
    scale = lax.rsqrt(jnp.maximum(variance, 0.0) + EPS)
    line_row = lax.broadcasted_iota(jnp.int32, (128, rows), 0)
    table = jnp.where(line_row == TP, scale, 0.0)
    head_row = lax.broadcasted_iota(jnp.int32, (128, width), 0)
    matrix = jnp.zeros((128, width), F32)
    for number in range(len(pieces)):
        table = jnp.where(line_row == number, firsts[number] * (1.0 / features) - average, table)
        matrix = jnp.where(head_row == number, heads[number], matrix)
    turned = table.T
    total = total + jnp.dot(
        turned, matrix, preferred_element_type=F32, precision=lax.Precision.HIGHEST
    )
    return total, turned[:, TP : TP + 1], offset


def cheap():
    return pl.CostEstimate(flops=1, bytes_accessed=1, transcendentals=0)


def stage_kernel(w_ref, x_ref, w_out, x_out, sems):
    copies = [
        pltpu.make_async_copy(w_ref, w_out, sems.at[0]),
        pltpu.make_async_copy(x_ref, x_out, sems.at[1]),
    ]
    for copy in copies:
        copy.start()
    for copy in copies:
        copy.wait()


def stage(w, x):
    return pl.pallas_call(
        stage_kernel,
        out_shape=[jax.ShapeDtypeStruct(w.shape, w.dtype), jax.ShapeDtypeStruct(x.shape, x.dtype)],
        in_specs=[HBM, HBM],
        out_specs=[HBM, HBM],
        scratch_shapes=[pltpu.SemaphoreType.DMA((2,))],
        compiler_params=params(4),
        cost_estimate=cheap(),
        name="stage",
    )(w, x)


def pick_kernel(place, own_ref, *refs):
    chip = place[2]
    out_ref = refs[-1]
    value = own_ref[...]
    for d in range(1, CHIPS):
        value = jnp.where(chip == d, refs[d - 1][...], value)
    out_ref[...] = value


def pick(place, own, received, after):
    return pl.pallas_call(
        pick_kernel,
        out_shape=jax.ShapeDtypeStruct(own.shape, own.dtype),
        in_specs=[SMEM] + [VMEM] * CHIPS + [HBM] * len(after),
        out_specs=VMEM,
        compiler_params=params(4),
        cost_estimate=cheap(),
        name="pick",
    )(place, own, *received, *after)


def qkv_kernel(layered, *refs):
    refs = list(refs)
    place, x_ref = refs.pop(0), refs.pop(0)
    pieces = [refs.pop(0) for _ in range(2)] if layered else []
    even_ref, odd_ref, w_ref = refs.pop(0), refs.pop(0), refs.pop(0)
    base_ref = refs.pop(0) if layered else None
    out_ref, lhs = refs
    core, layer = place[1], place[3]
    rows, columns = x_ref.shape
    width = w_ref.shape[2]

    vectors = jnp.where(core == 0, even_ref[...], odd_ref[...])
    gain, bias = vectors[0:1, :], vectors[1:2, :]
    row16 = lax.broadcasted_iota(jnp.int32, (EXTRA, columns), 0)
    tail = jnp.zeros((EXTRA, columns), F32)
    for number, vector in enumerate(split_parts(gain, 2) + split_parts(bias, 2)):
        tail = tail + jnp.where(row16 == number, vector, 0.0)
    lhs[rows : rows + EXTRA, :] = tail.astype(BF16)

    if layered:
        half_rows = rows // 2
        for half, piece in ((core, pieces[0]), (1 - core, pieces[1])):
            place_rows = pl.ds(pl.multiple_of(half * half_rows, half_rows), half_rows)
            tokens = x_ref[place_rows, :].astype(F32)
            added = tokens + piece[...].astype(F32)
            base_ref[place_rows, :] = jnp.where(layer == 1, added, tokens).astype(BF16)
    source = base_ref if layered else x_ref
    firsts, seconds = [], []
    for start, size in segments_of(rows):
        value = source[start : start + size, :].astype(F32)
        first = jnp.sum(value, axis=1, keepdims=True)
        second = jnp.sum(value * value, axis=1, keepdims=True)
        lhs[start : start + size, :] = ((value - first * (1.0 / columns)) * gain).astype(BF16)
        lane = lax.broadcasted_iota(jnp.int32, (size, 128), 1)
        turned = jnp.where(lane == 0, first, jnp.where(lane == 1, second, 0.0)).T
        firsts.append(turned[0:1, :])
        seconds.append(turned[1:2, :])
    blank = jnp.zeros((1, width), F32)
    joined = lambda lines: jnp.concatenate(lines, axis=1) if len(lines) > 1 else lines[0]
    lines = ending(blank, blank, joined(firsts), joined(seconds), width)
    out_row = lax.broadcasted_iota(jnp.int32, (EXTRA, width), 0)

    for pair in range(TP // 2):
        weights = jnp.concatenate([w_ref[2 * pair], w_ref[2 * pair + 1]], axis=1)
        result = jnp.dot(lhs[...], weights, preferred_element_type=F32)
        for side in range(2):
            head = 2 * pair + side
            part = result[:, side * width : (side + 1) * width]
            ends = part[rows : rows + EXTRA, :]
            table = lines
            vectors = split_parts(ends[0:1] + ends[1:2], 2) + split_parts(ends[2:3] + ends[3:4], 2)
            for number, vector in enumerate(vectors):
                table = table + jnp.where(out_row == number, vector, 0.0)
            out_ref[head, 0:rows, :] = part[0:rows, :].astype(BF16)
            out_ref[head, rows : rows + EXTRA, :] = table.astype(BF16)


def qkv(place, x, pieces, even, odd, w):
    rows, columns = x.shape
    heads, _, width = w.shape
    shapes = [jax.ShapeDtypeStruct((heads, rows + EXTRA, width), BF16)]
    if pieces:
        shapes = [jax.ShapeDtypeStruct((rows, columns), BF16)] + shapes
    out = pl.pallas_call(
        functools.partial(qkv_kernel, bool(pieces)),
        out_shape=shapes,
        in_specs=[SMEM] + [VMEM] * (len(pieces) + 4),
        out_specs=[VMEM] * len(shapes),
        scratch_shapes=[pltpu.VMEM((rows + EXTRA, columns), BF16)],
        compiler_params=params(24),
        cost_estimate=cheap(),
        name="qkv",
    )(place, x, *pieces, even, odd, w)
    return out if pieces else (None, out[0])


def attention_kernel(features, pieces_ref, out_ref):
    rows, head_dim = out_ref.shape
    total, scale, offset = combine([pieces_ref.at[t] for t in range(TP)], features // TP)
    joined = (total * scale + offset).astype(BF16)
    query = joined[:, :head_dim]
    key = joined[:, head_dim : 2 * head_dim]
    value = joined[:, 2 * head_dim :]
    scores = lax.dot_general(
        query, key, (((1,), (1,)), ((), ())), preferred_element_type=F32
    ) * (1.0 / head_dim**0.5)
    at_query = lax.broadcasted_iota(jnp.int32, (rows, rows), 0)
    at_key = lax.broadcasted_iota(jnp.int32, (rows, rows), 1)
    scores = jnp.where(at_key <= at_query, scores, -1e30)
    highest = jnp.max(scores, axis=1, keepdims=True)
    lifted = jnp.exp(scores - highest)
    weights = (lifted * (1.0 / jnp.sum(lifted, axis=1, keepdims=True))).astype(BF16)
    out_ref[...] = jnp.dot(weights, value, preferred_element_type=F32).astype(BF16)


def attention(pieces, features):
    rows = pieces.shape[1] - EXTRA
    head_dim = pieces.shape[2] // 3
    return pl.pallas_call(
        functools.partial(attention_kernel, features),
        out_shape=jax.ShapeDtypeStruct((rows, head_dim), BF16),
        in_specs=[VMEM],
        out_specs=VMEM,
        compiler_params=params(24),
        cost_estimate=cheap(),
        name="attention",
    )(pieces)


def project_kernel(passing, place, *refs):
    refs = list(refs)
    pieces = [refs.pop(0) for _ in range(TP)]
    w_ref = refs.pop(0)
    old = [refs.pop(0) for _ in range(2)] if passing else None
    keep_ref, send_ref, side = refs
    me, core, layer = place[0], place[1], place[3]
    rows, head_dim = pieces[0].shape

    def work():
        for d in range(TP):
            start = pl.multiple_of(jnp.bitwise_xor(me, d) * head_dim, head_dim)
            side[:, pl.ds(start, head_dim)] = pieces[d][...]
        for half, target in ((1 - core, send_ref), (core, keep_ref)):
            place_rows = pl.ds(pl.multiple_of(half * (rows // 2), rows // 2), rows // 2)
            target[...] = jnp.dot(
                side[place_rows, :], w_ref[...], preferred_element_type=F32
            ).astype(BF16)

    if passing:
        pl.when(layer == 1)(work)

        @pl.when(layer == 0)
        def _():
            keep_ref[...] = old[0][...]
            send_ref[...] = old[1][...]
    else:
        work()


def project(place, pieces, w, old):
    rows, head_dim = pieces[0].shape
    columns = w.shape[1]
    shape = jax.ShapeDtypeStruct((rows // 2, columns), BF16)
    old = list(old) if old else []
    return pl.pallas_call(
        functools.partial(project_kernel, bool(old)),
        out_shape=[shape] * 2,
        in_specs=[SMEM] + [VMEM] * (TP + 1 + len(old)),
        out_specs=[VMEM] * 2,
        scratch_shapes=[pltpu.VMEM((rows, TP * head_dim), BF16)],
        compiler_params=params(24),
        cost_estimate=cheap(),
        name="project",
    )(place, *pieces, w, *old)


def quarters_kernel(place, keep_ref, got_ref, *outs):
    chip = place[2]
    size = outs[0].shape[0]
    for d in range(CHIPS):
        rows = pl.ds(pl.multiple_of(jnp.bitwise_xor(chip, d) * size, size), size)
        outs[d][...] = (keep_ref[rows, :].astype(F32) + got_ref[rows, :].astype(F32)).astype(BF16)


def quarters(place, keep, got):
    rows, columns = keep.shape
    return pl.pallas_call(
        quarters_kernel,
        out_shape=[jax.ShapeDtypeStruct((rows // CHIPS, columns), BF16)] * CHIPS,
        in_specs=[SMEM, VMEM, VMEM],
        out_specs=[VMEM] * CHIPS,
        compiler_params=params(16),
        cost_estimate=cheap(),
        name="quarters",
    )(place, keep, got)


def arrange_kernel(place, *refs):
    chip = place[2]
    out_ref = refs[CHIPS]
    size = out_ref.shape[0] // CHIPS
    for d in range(CHIPS):
        rows = pl.ds(pl.multiple_of(jnp.bitwise_xor(chip, d) * size, size), size)
        out_ref[rows, :] = refs[d][...]


def arrange(place, pieces):
    rows, columns = pieces[0].shape
    return pl.pallas_call(
        arrange_kernel,
        out_shape=jax.ShapeDtypeStruct((rows * CHIPS, columns), BF16),
        in_specs=[SMEM] + [VMEM] * CHIPS,
        out_specs=VMEM,
        compiler_params=params(16),
        cost_estimate=cheap(),
        name="arrange",
    )(place, *pieces)


def finish_kernel(place, base_ref, keep_ref, got_ref, send_ref, other_keep_ref, own_ref, other_ref, out_ref):
    core = place[1]
    half_rows = keep_ref.shape[0]
    second = core.astype(F32)
    for half, sums, mine, theirs in (
        (core, own_ref, keep_ref, got_ref),
        (1 - core, other_ref, send_ref, other_keep_ref),
    ):
        rows = pl.ds(pl.multiple_of(half * half_rows, half_rows), half_rows)
        out_ref[rows, :] = (
            base_ref[rows, :].astype(F32)
            + sums[...].astype(F32)
            + mine[...].astype(F32)
            + second * theirs[...].astype(F32)
        ).astype(BF16)


def finish(place, base, *values):
    return pl.pallas_call(
        finish_kernel,
        out_shape=jax.ShapeDtypeStruct(base.shape, BF16),
        in_specs=[SMEM] + [VMEM] * (1 + len(values)),
        out_specs=VMEM,
        compiler_params=params(24),
        cost_estimate=cheap(),
        name="finish",
    )(place, base, *values)


def over_tp(value):
    return lax.all_to_all(value, "tp", 0, 0, tiled=True)


def over_cores(value):
    return lax.ppermute(value, "section", [(s, s ^ 1) for s in range(2 * SPAN)])


def over_chips(value, d):
    return lax.ppermute(value, "section", [(s, s ^ (2 * d)) for s in range(2 * SPAN)])


def spread(value):
    got = {0: value}
    for d in (5, 7, 3, 1, 4, 6, 2):
        got[d] = lax.ppermute(value, "tp", [(t, t ^ d) for t in range(TP)])
    return [got[d] for d in range(TP)]


def over_layer(values):
    return [values[0]] + [over_chips(values[d], d) for d in range(1, CHIPS)]


def on_device(tokens, ln_gain, ln_bias, w_qkv, w_out):
    section = lax.axis_index("section")
    me = lax.axis_index("tp")
    core = section % 2
    chip = (section // 2) % CHIPS
    layer = section // SPAN
    place = jnp.stack([me, core, chip, layer]).astype(jnp.int32)
    weight_in = w_qkv[0]
    weight_back = w_out[0]
    features = tokens.shape[1] * TP

    vectors = jnp.concatenate([ln_gain, ln_bias], axis=0)
    weight_in, tokens = stage(weight_in, tokens)
    received = [over_chips(vectors, d) for d in range(1, CHIPS)]
    even = pick(place, vectors, received, [weight_in])
    odd = over_cores(even)

    _, part = qkv(place, tokens, [], even, odd, weight_in)
    out = attention(over_tp(part), features)
    kept = project(place, spread(out), weight_back, None)
    keep, send = kept
    quarter = quarters(place, keep, over_cores(send))
    total = sum(value.astype(F32) for value in over_layer(quarter)).astype(BF16)
    half = arrange(place, over_layer([over_chips(total, CHIPS)] * CHIPS))

    base, part = qkv(place, tokens, [half, over_cores(half)], even, odd, weight_in)
    out = attention(over_tp(part), features)
    keep, send = project(place, spread(out), weight_back, kept)
    got = over_cores(send)
    other_keep = over_cores(keep)
    arrived = over_layer(quarters(place, keep, got))
    before = []
    for d in range(CHIPS):
        target = jnp.bitwise_xor(chip, d)
        before.append(
            sum(
                jnp.where(jnp.bitwise_xor(chip, e) < target, arrived[e].astype(F32), 0.0)
                for e in range(CHIPS)
            ).astype(BF16)
        )
    own = arrange(place, over_layer(before))
    return finish(place, base, keep, got, send, other_keep, own, over_cores(own))[None]


def solution(mesh):
    return jax.shard_map(
        on_device,
        mesh=mesh,
        in_specs=(
            P("dp", "tp"),
            P("section", "tp"),
            P("section", "tp"),
            P("section", None, "tp", None),
            P("section", None, "tp"),
        ),
        out_specs=P("section", "dp", "tp"),
        check_vma=False,
    )
```

```python
import functools

import jax
import jax.numpy as jnp
from jax import lax
from jax.experimental import pallas as pl
from jax.experimental.pallas import tpu as pltpu
from jax.sharding import PartitionSpec as P

SPAN = 8
TP = 8
CHIPS = 4
EXTRA = 16
EPS = 1e-05
SEGMENT = 256
BF16 = jnp.bfloat16
F32 = jnp.float32
VMEM = pl.BlockSpec(memory_space=pltpu.VMEM)
SMEM = pl.BlockSpec(memory_space=pltpu.SMEM)
HBM = pl.BlockSpec(memory_space=pl.ANY)


def params(mib):
    return pltpu.CompilerParams(vmem_limit_bytes=mib * 1024 * 1024)


def segments_of(rows):
    size = min(rows, SEGMENT)
    return [(start, size) for start in range(0, rows, size)]


def split_parts(value, count):
    parts = []
    for _ in range(count):
        part = value.astype(BF16).astype(F32)
        parts.append(part)
        value = value - part
    return parts


def ending(head_line, offset_line, first, second, width):
    vectors = split_parts(head_line, 2) + split_parts(offset_line, 2)
    for line in (first, second):
        for start, size in segments_of(line.shape[1]):
            for part in split_parts(line[:, start : start + size], 3):
                vectors.append(jnp.concatenate([part, jnp.zeros((1, width - size), F32)], axis=1))
    row = lax.broadcasted_iota(jnp.int32, (EXTRA, width), 0)
    table = jnp.zeros((EXTRA, width), F32)
    for number, vector in enumerate(vectors):
        table = table + jnp.where(row == number, vector, 0.0)
    return table


def combine(pieces, features):
    rows, width = pieces[0].shape[0] - EXTRA, pieces[0].shape[1]
    segments = segments_of(rows)
    total = jnp.zeros((rows, width), F32)
    heads, firsts, offset, second = [], [], 0.0, 0.0
    for piece in pieces:
        total = total + piece[0:rows, :].astype(F32)
        ends = piece[rows : rows + EXTRA, :].astype(F32)
        heads.append(ends[0:1] + ends[1:2])
        offset = offset + (ends[2:3] + ends[3:4])
        lines = []
        for kind in range(2):
            spans = []
            for number, (_, size) in enumerate(segments):
                slot = 4 + (kind * len(segments) + number) * 3
                spans.append((ends[slot : slot + 1] + ends[slot + 1 : slot + 2] + ends[slot + 2 : slot + 3])[:, :size])
            lines.append(jnp.concatenate(spans, axis=1) if len(spans) > 1 else spans[0])
        firsts.append(lines[0])
        second = second + lines[1]
    first = sum(firsts)
    count = features * len(pieces)
    average = first * (1.0 / count)
    variance = second * (1.0 / count) - average * average
    scale = lax.rsqrt(jnp.maximum(variance, 0.0) + EPS)
    line_row = lax.broadcasted_iota(jnp.int32, (128, rows), 0)
    table = jnp.where(line_row == TP, scale, 0.0)
    head_row = lax.broadcasted_iota(jnp.int32, (128, width), 0)
    matrix = jnp.zeros((128, width), F32)
    for number in range(len(pieces)):
        table = jnp.where(line_row == number, firsts[number] * (1.0 / features) - average, table)
        matrix = jnp.where(head_row == number, heads[number], matrix)
    turned = table.T
    total = total + jnp.dot(
        turned, matrix, preferred_element_type=F32, precision=lax.Precision.HIGHEST
    )
    return total, turned[:, TP : TP + 1], offset


def cheap():
    return pl.CostEstimate(flops=1, bytes_accessed=1, transcendentals=0)


def stage_kernel(w_ref, x_ref, w_out, x_out, sems):
    copies = [
        pltpu.make_async_copy(w_ref, w_out, sems.at[0]),
        pltpu.make_async_copy(x_ref, x_out, sems.at[1]),
    ]
    for copy in copies:
        copy.start()
    for copy in copies:
        copy.wait()


def stage(w, x):
    return pl.pallas_call(
        stage_kernel,
        out_shape=[jax.ShapeDtypeStruct(w.shape, w.dtype), jax.ShapeDtypeStruct(x.shape, x.dtype)],
        in_specs=[HBM, HBM],
        out_specs=[HBM, HBM],
        scratch_shapes=[pltpu.SemaphoreType.DMA((2,))],
        compiler_params=params(4),
        cost_estimate=cheap(),
        name="stage",
    )(w, x)


def pick_kernel(place, own_ref, *refs):
    chip = place[2]
    out_ref = refs[-1]
    value = own_ref[...]
    for d in range(1, CHIPS):
        value = jnp.where(chip == d, refs[d - 1][...], value)
    out_ref[...] = value


def pick(place, own, received, after):
    return pl.pallas_call(
        pick_kernel,
        out_shape=jax.ShapeDtypeStruct(own.shape, own.dtype),
        in_specs=[SMEM] + [VMEM] * CHIPS + [HBM] * len(after),
        out_specs=VMEM,
        compiler_params=params(4),
        cost_estimate=cheap(),
        name="pick",
    )(place, own, *received, *after)


def qkv_kernel(layered, *refs):
    refs = list(refs)
    place, x_ref = refs.pop(0), refs.pop(0)
    pieces = [refs.pop(0) for _ in range(2 * CHIPS)] if layered else []
    even_ref, odd_ref, w_ref = refs.pop(0), refs.pop(0), refs.pop(0)
    base_ref = refs.pop(0) if layered else None
    out_ref, lhs = refs
    core, chip, layer = place[1], place[2], place[3]
    rows, columns = x_ref.shape
    width = w_ref.shape[2]

    if layered:
        size = rows // (2 * CHIPS)
        for number, piece in enumerate(pieces):
            half = core if number < CHIPS else 1 - core
            start = (half * CHIPS + jnp.bitwise_xor(chip, number % CHIPS)) * size
            place_rows = pl.ds(pl.multiple_of(start, size), size)
            tokens = x_ref[place_rows, :].astype(F32)
            added = tokens + piece[...].astype(F32)
            base_ref[place_rows, :] = jnp.where(layer == 1, added, tokens).astype(BF16)
    @pl.when(layer == (1 if layered else 0))
    def _():
        vectors = jnp.where(core == 0, even_ref[...], odd_ref[...])
        gain, bias = vectors[0:1, :], vectors[1:2, :]
        row16 = lax.broadcasted_iota(jnp.int32, (EXTRA, columns), 0)
        tail = jnp.zeros((EXTRA, columns), F32)
        for number, vector in enumerate(split_parts(gain, 2) + split_parts(bias, 2)):
            tail = tail + jnp.where(row16 == number, vector, 0.0)
        lhs[rows : rows + EXTRA, :] = tail.astype(BF16)

        source = base_ref if layered else x_ref
        firsts, seconds = [], []
        for start, size in segments_of(rows):
            value = source[start : start + size, :].astype(F32)
            first = jnp.sum(value, axis=1, keepdims=True)
            second = jnp.sum(value * value, axis=1, keepdims=True)
            lhs[start : start + size, :] = ((value - first * (1.0 / columns)) * gain).astype(BF16)
            lane = lax.broadcasted_iota(jnp.int32, (size, 128), 1)
            turned = jnp.where(lane == 0, first, jnp.where(lane == 1, second, 0.0)).T
            firsts.append(turned[0:1, :])
            seconds.append(turned[1:2, :])
        blank = jnp.zeros((1, width), F32)
        joined = lambda lines: jnp.concatenate(lines, axis=1) if len(lines) > 1 else lines[0]
        lines = ending(blank, blank, joined(firsts), joined(seconds), width)
        out_row = lax.broadcasted_iota(jnp.int32, (EXTRA, width), 0)

        for pair in range(TP // 2):
            weights = jnp.concatenate([w_ref[2 * pair], w_ref[2 * pair + 1]], axis=1)
            result = jnp.dot(lhs[...], weights, preferred_element_type=F32)
            for side in range(2):
                head = 2 * pair + side
                part = result[:, side * width : (side + 1) * width]
                ends = part[rows : rows + EXTRA, :]
                table = lines
                vectors = split_parts(ends[0:1] + ends[1:2], 2) + split_parts(ends[2:3] + ends[3:4], 2)
                for number, vector in enumerate(vectors):
                    table = table + jnp.where(out_row == number, vector, 0.0)
                out_ref[head, 0:rows, :] = part[0:rows, :].astype(BF16)
                out_ref[head, rows : rows + EXTRA, :] = table.astype(BF16)


def qkv(place, x, pieces, even, odd, w):
    rows, columns = x.shape
    heads, _, width = w.shape
    shapes = [jax.ShapeDtypeStruct((heads, rows + EXTRA, width), BF16)]
    if pieces:
        shapes = [jax.ShapeDtypeStruct((rows, columns), BF16)] + shapes
    out = pl.pallas_call(
        functools.partial(qkv_kernel, bool(pieces)),
        out_shape=shapes,
        in_specs=[SMEM] + [VMEM] * (len(pieces) + 4),
        out_specs=[VMEM] * len(shapes),
        scratch_shapes=[pltpu.VMEM((rows + EXTRA, columns), BF16)],
        compiler_params=params(24),
        cost_estimate=cheap(),
        name="qkv",
    )(place, x, *pieces, even, odd, w)
    return out if pieces else (None, out[0])


def attention_kernel(features, phase, place, pieces_ref, out_ref):
    rows, head_dim = out_ref.shape

    @pl.when(place[3] == phase)
    def _():
        total, scale, offset = combine([pieces_ref.at[t] for t in range(TP)], features // TP)
        joined = (total * scale + offset).astype(BF16)
        query = joined[:, :head_dim]
        key = joined[:, head_dim : 2 * head_dim]
        value = joined[:, 2 * head_dim :]
        scores = lax.dot_general(
            query, key, (((1,), (1,)), ((), ())), preferred_element_type=F32
        ) * (1.0 / head_dim**0.5)
        at_query = lax.broadcasted_iota(jnp.int32, (rows, rows), 0)
        at_key = lax.broadcasted_iota(jnp.int32, (rows, rows), 1)
        scores = jnp.where(at_key <= at_query, scores, -1e30)
        highest = jnp.max(scores, axis=1, keepdims=True)
        lifted = jnp.exp(scores - highest)
        weights = (lifted * (1.0 / jnp.sum(lifted, axis=1, keepdims=True))).astype(BF16)
        out_ref[...] = jnp.dot(weights, value, preferred_element_type=F32).astype(BF16)


def attention(place, pieces, features, phase):
    rows = pieces.shape[1] - EXTRA
    head_dim = pieces.shape[2] // 3
    return pl.pallas_call(
        functools.partial(attention_kernel, features, phase),
        out_shape=jax.ShapeDtypeStruct((rows, head_dim), BF16),
        in_specs=[SMEM, VMEM],
        out_specs=VMEM,
        compiler_params=params(24),
        cost_estimate=cheap(),
        name="attention",
    )(place, pieces)


def project_kernel(passing, place, *refs):
    refs = list(refs)
    pieces = [refs.pop(0) for _ in range(TP)]
    w_ref = refs.pop(0)
    old = [refs.pop(0) for _ in range(2)] if passing else None
    keep_ref, send_ref, side = refs
    me, core, layer = place[0], place[1], place[3]
    rows, head_dim = pieces[0].shape

    def work():
        for d in range(TP):
            start = pl.multiple_of(jnp.bitwise_xor(me, d) * head_dim, head_dim)
            side[:, pl.ds(start, head_dim)] = pieces[d][...]
        for half, target in ((1 - core, send_ref), (core, keep_ref)):
            place_rows = pl.ds(pl.multiple_of(half * (rows // 2), rows // 2), rows // 2)
            target[...] = jnp.dot(
                side[place_rows, :], w_ref[...], preferred_element_type=F32
            ).astype(BF16)

    if passing:
        pl.when(layer == 1)(work)

        @pl.when(layer == 0)
        def _():
            keep_ref[...] = old[0][...]
            send_ref[...] = old[1][...]
    else:
        work()


def project(place, pieces, w, old):
    rows, head_dim = pieces[0].shape
    columns = w.shape[1]
    shape = jax.ShapeDtypeStruct((rows // 2, columns), BF16)
    old = list(old) if old else []
    return pl.pallas_call(
        functools.partial(project_kernel, bool(old)),
        out_shape=[shape] * 2,
        in_specs=[SMEM] + [VMEM] * (TP + 1 + len(old)),
        out_specs=[VMEM] * 2,
        scratch_shapes=[pltpu.VMEM((rows, TP * head_dim), BF16)],
        compiler_params=params(24),
        cost_estimate=cheap(),
        name="project",
    )(place, *pieces, w, *old)


def quarters_kernel(place, keep_ref, got_ref, *outs):
    chip = place[2]
    size = outs[0].shape[0]
    for d in range(CHIPS):
        rows = pl.ds(pl.multiple_of(jnp.bitwise_xor(chip, d) * size, size), size)
        outs[d][...] = (keep_ref[rows, :].astype(F32) + got_ref[rows, :].astype(F32)).astype(BF16)


def quarters(place, keep, got):
    rows, columns = keep.shape
    return pl.pallas_call(
        quarters_kernel,
        out_shape=[jax.ShapeDtypeStruct((rows // CHIPS, columns), BF16)] * CHIPS,
        in_specs=[SMEM, VMEM, VMEM],
        out_specs=[VMEM] * CHIPS,
        compiler_params=params(16),
        cost_estimate=cheap(),
        name="quarters",
    )(place, keep, got)


def finish_kernel(place, base_ref, keep_ref, got_ref, send_ref, other_keep_ref, *refs):
    own, others, out_ref = refs[:CHIPS], refs[CHIPS : 2 * CHIPS], refs[2 * CHIPS]
    core, chip = place[1], place[2]
    half_rows = keep_ref.shape[0]
    size = half_rows // CHIPS
    second = core.astype(F32)
    for half, sums, mine, theirs in (
        (core, own, keep_ref, got_ref),
        (1 - core, others, send_ref, other_keep_ref),
    ):
        for d in range(CHIPS):
            start = pl.multiple_of(jnp.bitwise_xor(chip, d) * size, size)
            inside = pl.ds(start, size)
            whole = pl.ds(pl.multiple_of(half * half_rows + start, size), size)
            out_ref[whole, :] = (
                base_ref[whole, :].astype(F32)
                + sums[d][...].astype(F32)
                + mine[inside, :].astype(F32)
                + second * theirs[inside, :].astype(F32)
            ).astype(BF16)


def finish(place, base, keep, got, send, other_keep, own, others):
    return pl.pallas_call(
        finish_kernel,
        out_shape=jax.ShapeDtypeStruct(base.shape, BF16),
        in_specs=[SMEM] + [VMEM] * (5 + 2 * CHIPS),
        out_specs=VMEM,
        compiler_params=params(24),
        cost_estimate=cheap(),
        name="finish",
    )(place, base, keep, got, send, other_keep, *own, *others)


def over_tp(value):
    return lax.all_to_all(value, "tp", 0, 0, tiled=True)


def over_cores(value):
    return lax.ppermute(value, "section", [(s, s ^ 1) for s in range(2 * SPAN)])


def over_chips(value, d):
    return lax.ppermute(value, "section", [(s, s ^ (2 * d)) for s in range(2 * SPAN)])


def spread(value):
    got = {0: value}
    for d in (5, 7, 3, 1, 4, 6, 2):
        got[d] = lax.ppermute(value, "tp", [(t, t ^ d) for t in range(TP)])
    return [got[d] for d in range(TP)]


def over_layer(values):
    return [values[0]] + [over_chips(values[d], d) for d in range(1, CHIPS)]


def on_device(tokens, ln_gain, ln_bias, w_qkv, w_out):
    section = lax.axis_index("section")
    me = lax.axis_index("tp")
    core = section % 2
    chip = (section // 2) % CHIPS
    layer = section // SPAN
    place = jnp.stack([me, core, chip, layer]).astype(jnp.int32)
    weight_in = w_qkv[0]
    weight_back = w_out[0]
    features = tokens.shape[1] * TP

    vectors = jnp.concatenate([ln_gain, ln_bias], axis=0)
    weight_in, tokens = stage(weight_in, tokens)
    received = [over_chips(vectors, d) for d in range(1, CHIPS)]
    even = pick(place, vectors, received, [weight_in])
    odd = over_cores(even)

    _, part = qkv(place, tokens, [], even, odd, weight_in)
    out = attention(place, over_tp(part), features, 0)
    kept = project(place, spread(out), weight_back, None)
    keep, send = kept
    arrived = over_layer(quarters(place, keep, over_cores(send)))
    total = sum(value.astype(F32) for value in arrived).astype(BF16)
    own = over_layer([over_chips(total, CHIPS)] * CHIPS)
    others = [over_cores(value) for value in own]

    base, part = qkv(place, tokens, own + others, even, odd, weight_in)
    out = attention(place, over_tp(part), features, 1)
    keep, send = project(place, spread(out), weight_back, kept)
    got = over_cores(send)
    other_keep = over_cores(keep)
    arrived = over_layer(quarters(place, keep, got))
    before = []
    for d in range(CHIPS):
        target = jnp.bitwise_xor(chip, d)
        before.append(
            sum(
                jnp.where(jnp.bitwise_xor(chip, e) < target, arrived[e].astype(F32), 0.0)
                for e in range(CHIPS)
            ).astype(BF16)
        )
    own = over_layer(before)
    others = [over_cores(value) for value in own]
    return finish(place, base, keep, got, send, other_keep, own, others)[None]


def solution(mesh):
    return jax.shard_map(
        on_device,
        mesh=mesh,
        in_specs=(
            P("dp", "tp"),
            P("section", "tp"),
            P("section", "tp"),
            P("section", None, "tp", None),
            P("section", None, "tp"),
        ),
        out_specs=P("section", "dp", "tp"),
        check_vma=False,
    )
```

```python
import functools

import jax
import jax.numpy as jnp
from jax import lax
from jax.experimental import pallas as pl
from jax.experimental.pallas import tpu as pltpu
from jax.sharding import PartitionSpec as P

SPAN = 8
TP = 8
CHIPS = 4
EXTRA = 16
EPS = 1e-05
ROUND = (0, 2, 3, 1)
AWAY = (0, 5, 7, 3, 1, 4, 6, 2)
SEGMENT = 256
BF16 = jnp.bfloat16
F32 = jnp.float32
VMEM = pl.BlockSpec(memory_space=pltpu.VMEM)
SMEM = pl.BlockSpec(memory_space=pltpu.SMEM)
HBM = pl.BlockSpec(memory_space=pl.ANY)


def params(mib):
    return pltpu.CompilerParams(vmem_limit_bytes=mib * 1024 * 1024)


def segments_of(rows):
    size = min(rows, SEGMENT)
    return [(start, size) for start in range(0, rows, size)]


def split_parts(value, count):
    parts = []
    for _ in range(count):
        part = value.astype(BF16).astype(F32)
        parts.append(part)
        value = value - part
    return parts


def ending(head_line, offset_line, first, second, width):
    vectors = split_parts(head_line, 2) + split_parts(offset_line, 2)
    for line in (first, second):
        for start, size in segments_of(line.shape[1]):
            for part in split_parts(line[:, start : start + size], 3):
                vectors.append(jnp.concatenate([part, jnp.zeros((1, width - size), F32)], axis=1))
    row = lax.broadcasted_iota(jnp.int32, (EXTRA, width), 0)
    table = jnp.zeros((EXTRA, width), F32)
    for number, vector in enumerate(vectors):
        table = table + jnp.where(row == number, vector, 0.0)
    return table


def combine(pieces, features):
    rows, width = pieces[0].shape[0] - EXTRA, pieces[0].shape[1]
    segments = segments_of(rows)
    total = jnp.zeros((rows, width), F32)
    heads, firsts, offset, second = [], [], 0.0, 0.0
    for piece in pieces:
        total = total + piece[0:rows, :].astype(F32)
        ends = piece[rows : rows + EXTRA, :].astype(F32)
        heads.append(ends[0:1] + ends[1:2])
        offset = offset + (ends[2:3] + ends[3:4])
        lines = []
        for kind in range(2):
            spans = []
            for number, (_, size) in enumerate(segments):
                slot = 4 + (kind * len(segments) + number) * 3
                spans.append((ends[slot : slot + 1] + ends[slot + 1 : slot + 2] + ends[slot + 2 : slot + 3])[:, :size])
            lines.append(jnp.concatenate(spans, axis=1) if len(spans) > 1 else spans[0])
        firsts.append(lines[0])
        second = second + lines[1]
    first = sum(firsts)
    count = features * len(pieces)
    average = first * (1.0 / count)
    variance = second * (1.0 / count) - average * average
    scale = lax.rsqrt(jnp.maximum(variance, 0.0) + EPS)
    line_row = lax.broadcasted_iota(jnp.int32, (128, rows), 0)
    table = jnp.where(line_row == TP, scale, 0.0)
    head_row = lax.broadcasted_iota(jnp.int32, (128, width), 0)
    matrix = jnp.zeros((128, width), F32)
    for number in range(len(pieces)):
        table = jnp.where(line_row == number, firsts[number] * (1.0 / features) - average, table)
        matrix = jnp.where(head_row == number, heads[number], matrix)
    turned = table.T
    total = total + jnp.dot(
        turned, matrix, preferred_element_type=F32, precision=lax.Precision.HIGHEST
    )
    return total, turned[:, TP : TP + 1], offset


def cheap():
    return pl.CostEstimate(flops=1, bytes_accessed=1, transcendentals=0)


def stage_kernel(w_ref, x_ref, w_out, x_out, sems):
    copies = [
        pltpu.make_async_copy(w_ref, w_out, sems.at[0]),
        pltpu.make_async_copy(x_ref, x_out, sems.at[1]),
    ]
    for copy in copies:
        copy.start()
    for copy in copies:
        copy.wait()


def stage(w, x):
    return pl.pallas_call(
        stage_kernel,
        out_shape=[jax.ShapeDtypeStruct(w.shape, w.dtype), jax.ShapeDtypeStruct(x.shape, x.dtype)],
        in_specs=[HBM, HBM],
        out_specs=[HBM, HBM],
        scratch_shapes=[pltpu.SemaphoreType.DMA((2,))],
        compiler_params=params(4),
        cost_estimate=cheap(),
        name="stage",
    )(w, x)


def pick_kernel(place, own_ref, *refs):
    chip = place[2]
    out_ref = refs[-1]
    value = own_ref[...]
    for d in range(1, CHIPS):
        value = jnp.where(chip == d, refs[d - 1][...], value)
    out_ref[...] = value


def pick(place, own, received, after):
    return pl.pallas_call(
        pick_kernel,
        out_shape=jax.ShapeDtypeStruct(own.shape, own.dtype),
        in_specs=[SMEM] + [VMEM] * CHIPS + [HBM] * len(after),
        out_specs=VMEM,
        compiler_params=params(4),
        cost_estimate=cheap(),
        name="pick",
    )(place, own, *received, *after)


def qkv_kernel(layered, *refs):
    refs = list(refs)
    place, x_ref = refs.pop(0), refs.pop(0)
    pieces = [refs.pop(0) for _ in range(2 * CHIPS)] if layered else []
    even_ref, odd_ref, w_ref = refs.pop(0), refs.pop(0), refs.pop(0)
    base_ref = refs.pop(0) if layered else None
    out_ref, lhs = refs
    core, chip, layer = place[1], place[2], place[3]
    rows, columns = x_ref.shape
    width = w_ref.shape[2]

    if layered:
        size = rows // (2 * CHIPS)
        for number, piece in enumerate(pieces):
            half = core if number < CHIPS else 1 - core
            quarter = jnp.bitwise_xor(chip, ROUND[number % CHIPS] ^ (CHIPS - 1))
            start = (half * CHIPS + quarter) * size
            place_rows = pl.ds(pl.multiple_of(start, size), size)
            tokens = x_ref[place_rows, :].astype(F32)
            added = tokens + piece[...].astype(F32)
            base_ref[place_rows, :] = jnp.where(layer == 1, added, tokens).astype(BF16)
    @pl.when(layer == (1 if layered else 0))
    def _():
        vectors = jnp.where(core == 0, even_ref[...], odd_ref[...])
        gain, bias = vectors[0:1, :], vectors[1:2, :]
        row16 = lax.broadcasted_iota(jnp.int32, (EXTRA, columns), 0)
        tail = jnp.zeros((EXTRA, columns), F32)
        for number, vector in enumerate(split_parts(gain, 2) + split_parts(bias, 2)):
            tail = tail + jnp.where(row16 == number, vector, 0.0)
        lhs[rows : rows + EXTRA, :] = tail.astype(BF16)

        source = base_ref if layered else x_ref
        firsts, seconds = [], []
        for start, size in segments_of(rows):
            value = source[start : start + size, :].astype(F32)
            first = jnp.sum(value, axis=1, keepdims=True)
            second = jnp.sum(value * value, axis=1, keepdims=True)
            lhs[start : start + size, :] = ((value - first * (1.0 / columns)) * gain).astype(BF16)
            lane = lax.broadcasted_iota(jnp.int32, (size, 128), 1)
            turned = jnp.where(lane == 0, first, jnp.where(lane == 1, second, 0.0)).T
            firsts.append(turned[0:1, :])
            seconds.append(turned[1:2, :])
        blank = jnp.zeros((1, width), F32)
        joined = lambda lines: jnp.concatenate(lines, axis=1) if len(lines) > 1 else lines[0]
        lines = ending(blank, blank, joined(firsts), joined(seconds), width)
        out_row = lax.broadcasted_iota(jnp.int32, (EXTRA, width), 0)

        for pair in range(TP // 2):
            weights = jnp.concatenate([w_ref[2 * pair], w_ref[2 * pair + 1]], axis=1)
            result = jnp.dot(lhs[...], weights, preferred_element_type=F32)
            for side in range(2):
                head = 2 * pair + side
                part = result[:, side * width : (side + 1) * width]
                ends = part[rows : rows + EXTRA, :]
                table = lines
                vectors = split_parts(ends[0:1] + ends[1:2], 2) + split_parts(ends[2:3] + ends[3:4], 2)
                for number, vector in enumerate(vectors):
                    table = table + jnp.where(out_row == number, vector, 0.0)
                out_ref[head, 0:rows, :] = part[0:rows, :].astype(BF16)
                out_ref[head, rows : rows + EXTRA, :] = table.astype(BF16)


def qkv(place, x, pieces, even, odd, w):
    rows, columns = x.shape
    heads, _, width = w.shape
    shapes = [jax.ShapeDtypeStruct((heads, rows + EXTRA, width), BF16)]
    if pieces:
        shapes = [jax.ShapeDtypeStruct((rows, columns), BF16)] + shapes
    out = pl.pallas_call(
        functools.partial(qkv_kernel, bool(pieces)),
        out_shape=shapes,
        in_specs=[SMEM] + [VMEM] * (len(pieces) + 4),
        out_specs=[VMEM] * len(shapes),
        scratch_shapes=[pltpu.VMEM((rows + EXTRA, columns), BF16)],
        compiler_params=params(24),
        cost_estimate=cheap(),
        name="qkv",
    )(place, x, *pieces, even, odd, w)
    return out if pieces else (None, out[0])


def attention_kernel(features, phase, place, pieces_ref, out_ref):
    rows, head_dim = out_ref.shape

    @pl.when(place[3] == phase)
    def _():
        total, scale, offset = combine([pieces_ref.at[t] for t in range(TP)], features // TP)
        joined = (total * scale + offset).astype(BF16)
        query = joined[:, :head_dim]
        key = joined[:, head_dim : 2 * head_dim]
        value = joined[:, 2 * head_dim :]
        scores = lax.dot_general(
            query, key, (((1,), (1,)), ((), ())), preferred_element_type=F32
        ) * (1.0 / head_dim**0.5)
        at_query = lax.broadcasted_iota(jnp.int32, (rows, rows), 0)
        at_key = lax.broadcasted_iota(jnp.int32, (rows, rows), 1)
        scores = jnp.where(at_key <= at_query, scores, -1e30)
        highest = jnp.max(scores, axis=1, keepdims=True)
        lifted = jnp.exp(scores - highest)
        weights = (lifted * (1.0 / jnp.sum(lifted, axis=1, keepdims=True))).astype(BF16)
        out_ref[...] = jnp.dot(weights, value, preferred_element_type=F32).astype(BF16)


def attention(place, pieces, features, phase):
    rows = pieces.shape[1] - EXTRA
    head_dim = pieces.shape[2] // 3
    return pl.pallas_call(
        functools.partial(attention_kernel, features, phase),
        out_shape=jax.ShapeDtypeStruct((rows, head_dim), BF16),
        in_specs=[SMEM, VMEM],
        out_specs=VMEM,
        compiler_params=params(24),
        cost_estimate=cheap(),
        name="attention",
    )(place, pieces)


def project_kernel(keeping, passing, place, *refs):
    refs = list(refs)
    pieces = [refs.pop(0) for _ in range(TP)]
    w_ref = refs.pop(0)
    old_ref = refs.pop(0) if passing else None
    out_ref, side = refs
    me, core, layer = place[0], place[1], place[3]
    rows, head_dim = out_ref.shape[0], pieces[0].shape[1]

    @pl.when(layer == (1 if passing else 0))
    def _():
        half = core if keeping else 1 - core
        inside = pl.ds(pl.multiple_of(half * rows, rows), rows)
        for d, piece in zip(AWAY, pieces):
            start = pl.multiple_of(jnp.bitwise_xor(me, d) * head_dim, head_dim)
            side[:, pl.ds(start, head_dim)] = piece[inside, :]
        out_ref[...] = jnp.dot(side[...], w_ref[...], preferred_element_type=F32).astype(BF16)

    if passing:

        @pl.when(layer == 0)
        def _():
            out_ref[...] = old_ref[...]


def project(keeping, place, pieces, w, old):
    rows, head_dim = pieces[0].shape
    columns = w.shape[1]
    return pl.pallas_call(
        functools.partial(project_kernel, keeping, bool(old)),
        out_shape=jax.ShapeDtypeStruct((rows // 2, columns), BF16),
        in_specs=[SMEM] + [VMEM] * (TP + 1 + len(old)),
        out_specs=VMEM,
        scratch_shapes=[pltpu.VMEM((rows // 2, TP * head_dim), BF16)],
        compiler_params=params(16),
        cost_estimate=cheap(),
        name="project",
    )(place, *pieces, w, *old)


def quarters_kernel(place, keep_ref, got_ref, *outs):
    chip = place[2]
    size = outs[0].shape[0]
    for d, out_ref in zip(ROUND, outs):
        rows = pl.ds(pl.multiple_of(jnp.bitwise_xor(chip, d) * size, size), size)
        out_ref[...] = (keep_ref[rows, :].astype(F32) + got_ref[rows, :].astype(F32)).astype(BF16)


def quarters(place, keep, got):
    rows, columns = keep.shape
    return pl.pallas_call(
        quarters_kernel,
        out_shape=[jax.ShapeDtypeStruct((rows // CHIPS, columns), BF16)] * CHIPS,
        in_specs=[SMEM, VMEM, VMEM],
        out_specs=[VMEM] * CHIPS,
        compiler_params=params(16),
        cost_estimate=cheap(),
        name="quarters",
    )(place, keep, got)


def finish_kernel(place, base_ref, keep_ref, got_ref, send_ref, other_keep_ref, *refs):
    own, others, out_ref = refs[:CHIPS], refs[CHIPS : 2 * CHIPS], refs[2 * CHIPS]
    core, chip = place[1], place[2]
    half_rows = keep_ref.shape[0]
    size = half_rows // CHIPS
    second = core.astype(F32)
    for half, sums, mine, theirs in (
        (core, own, keep_ref, got_ref),
        (1 - core, others, send_ref, other_keep_ref),
    ):
        for slot, d in enumerate(ROUND):
            start = pl.multiple_of(jnp.bitwise_xor(chip, d) * size, size)
            inside = pl.ds(start, size)
            whole = pl.ds(pl.multiple_of(half * half_rows + start, size), size)
            out_ref[whole, :] = (
                base_ref[whole, :].astype(F32)
                + sums[slot][...].astype(F32)
                + mine[inside, :].astype(F32)
                + second * theirs[inside, :].astype(F32)
            ).astype(BF16)


def finish(place, base, keep, got, send, other_keep, own, others):
    return pl.pallas_call(
        finish_kernel,
        out_shape=jax.ShapeDtypeStruct(base.shape, BF16),
        in_specs=[SMEM] + [VMEM] * (5 + 2 * CHIPS),
        out_specs=VMEM,
        compiler_params=params(24),
        cost_estimate=cheap(),
        name="finish",
    )(place, base, keep, got, send, other_keep, *own, *others)


def over_tp(value):
    return lax.all_to_all(value, "tp", 0, 0, tiled=True)


def over_cores(value):
    return lax.ppermute(value, "section", [(s, s ^ 1) for s in range(2 * SPAN)])


def over_chips(value, d):
    return lax.ppermute(value, "section", [(s, s ^ (2 * d)) for s in range(2 * SPAN)])


def spread(value):
    return [
        lax.ppermute(value, "tp", [(t, t ^ d) for t in range(TP)]) if d else value for d in AWAY
    ]


def over_layer(values):
    return [over_chips(value, d) if d else value for d, value in zip(ROUND, values)]


def on_device(tokens, ln_gain, ln_bias, w_qkv, w_out):
    section = lax.axis_index("section")
    me = lax.axis_index("tp")
    core = section % 2
    chip = (section // 2) % CHIPS
    layer = section // SPAN
    place = jnp.stack([me, core, chip, layer]).astype(jnp.int32)
    weight_in = w_qkv[0]
    weight_back = w_out[0]
    features = tokens.shape[1] * TP

    vectors = jnp.concatenate([ln_gain, ln_bias], axis=0)
    weight_in, tokens = stage(weight_in, tokens)
    received = [over_chips(vectors, d) for d in range(1, CHIPS)]
    even = pick(place, vectors, received, [weight_in])
    odd = over_cores(even)

    _, part = qkv(place, tokens, [], even, odd, weight_in)
    out = attention(place, over_tp(part), features, 0)
    heads = spread(out)
    send = project(False, place, heads, weight_back, [])
    got = over_cores(send)
    keep = project(True, place, heads, weight_back, [])
    arrived = over_layer(quarters(place, keep, got))
    total = sum(value.astype(F32) for value in arrived).astype(BF16)
    own = over_layer([over_chips(total, 2 * CHIPS - 1)] * CHIPS)
    others = [over_cores(value) for value in own]

    base, part = qkv(place, tokens, own + others, even, odd, weight_in)
    out = attention(place, over_tp(part), features, 1)
    heads = spread(out)
    send = project(False, place, heads, weight_back, [send])
    got = over_cores(send)
    keep = project(True, place, heads, weight_back, [keep])
    other_keep = over_cores(keep)
    arrived = over_layer(quarters(place, keep, got))
    before = []
    for d in ROUND:
        target = jnp.bitwise_xor(chip, d)
        before.append(
            sum(
                jnp.where(jnp.bitwise_xor(chip, e) < target, value.astype(F32), 0.0)
                for e, value in zip(ROUND, arrived)
            ).astype(BF16)
        )
    own = over_layer(before)
    others = [over_cores(value) for value in own]
    return finish(place, base, keep, got, send, other_keep, own, others)[None]


def solution(mesh):
    return jax.shard_map(
        on_device,
        mesh=mesh,
        in_specs=(
            P("dp", "tp"),
            P("section", "tp"),
            P("section", "tp"),
            P("section", None, "tp", None),
            P("section", None, "tp"),
        ),
        out_specs=P("section", "dp", "tp"),
        check_vma=False,
    )
```

```python
import functools

import jax
import jax.numpy as jnp
from jax import lax
from jax.experimental import pallas as pl
from jax.experimental.pallas import tpu as pltpu
from jax.sharding import PartitionSpec as P

SPAN = 8
TP = 8
CHIPS = 4
EXTRA = 16
EPS = 1e-05
ROUND = (0, 2, 3, 1)
AWAY = (0, 5, 7, 3, 1, 4, 6, 2)
SEGMENT = 256
BF16 = jnp.bfloat16
F32 = jnp.float32
VMEM = pl.BlockSpec(memory_space=pltpu.VMEM)
SMEM = pl.BlockSpec(memory_space=pltpu.SMEM)
HBM = pl.BlockSpec(memory_space=pl.ANY)


def params(mib):
    return pltpu.CompilerParams(vmem_limit_bytes=mib * 1024 * 1024)


def segments_of(rows):
    size = min(rows, SEGMENT)
    return [(start, size) for start in range(0, rows, size)]


def split_parts(value, count):
    parts = []
    for _ in range(count):
        part = value.astype(BF16).astype(F32)
        parts.append(part)
        value = value - part
    return parts


def ending(head_line, offset_line, first, second, width):
    vectors = split_parts(head_line, 2) + split_parts(offset_line, 2)
    for line in (first, second):
        for start, size in segments_of(line.shape[1]):
            for part in split_parts(line[:, start : start + size], 3):
                vectors.append(jnp.concatenate([part, jnp.zeros((1, width - size), F32)], axis=1))
    row = lax.broadcasted_iota(jnp.int32, (EXTRA, width), 0)
    table = jnp.zeros((EXTRA, width), F32)
    for number, vector in enumerate(vectors):
        table = table + jnp.where(row == number, vector, 0.0)
    return table


def combine(pieces, features):
    rows, width = pieces[0].shape[0] - EXTRA, pieces[0].shape[1]
    segments = segments_of(rows)
    total = jnp.zeros((rows, width), F32)
    heads, firsts, offset, second = [], [], 0.0, 0.0
    for piece in pieces:
        total = total + piece[0:rows, :].astype(F32)
        ends = piece[rows : rows + EXTRA, :].astype(F32)
        heads.append(ends[0:1] + ends[1:2])
        offset = offset + (ends[2:3] + ends[3:4])
        lines = []
        for kind in range(2):
            spans = []
            for number, (_, size) in enumerate(segments):
                slot = 4 + (kind * len(segments) + number) * 3
                spans.append((ends[slot : slot + 1] + ends[slot + 1 : slot + 2] + ends[slot + 2 : slot + 3])[:, :size])
            lines.append(jnp.concatenate(spans, axis=1) if len(spans) > 1 else spans[0])
        firsts.append(lines[0])
        second = second + lines[1]
    first = sum(firsts)
    count = features * len(pieces)
    average = first * (1.0 / count)
    variance = second * (1.0 / count) - average * average
    scale = lax.rsqrt(jnp.maximum(variance, 0.0) + EPS)
    line_row = lax.broadcasted_iota(jnp.int32, (128, rows), 0)
    table = jnp.where(line_row == TP, scale, 0.0)
    head_row = lax.broadcasted_iota(jnp.int32, (128, width), 0)
    matrix = jnp.zeros((128, width), F32)
    for number in range(len(pieces)):
        table = jnp.where(line_row == number, firsts[number] * (1.0 / features) - average, table)
        matrix = jnp.where(head_row == number, heads[number], matrix)
    turned = table.T
    total = total + jnp.dot(
        turned, matrix, preferred_element_type=F32, precision=lax.Precision.HIGHEST
    )
    return total, turned[:, TP : TP + 1], offset


def cheap():
    return pl.CostEstimate(flops=1, bytes_accessed=1, transcendentals=0)


def stage_kernel(w_ref, x_ref, w_out, x_out, sems):
    copies = [
        pltpu.make_async_copy(w_ref, w_out, sems.at[0]),
        pltpu.make_async_copy(x_ref, x_out, sems.at[1]),
    ]
    for copy in copies:
        copy.start()
    for copy in copies:
        copy.wait()


def stage(w, x):
    return pl.pallas_call(
        stage_kernel,
        out_shape=[jax.ShapeDtypeStruct(w.shape, w.dtype), jax.ShapeDtypeStruct(x.shape, x.dtype)],
        in_specs=[HBM, HBM],
        out_specs=[HBM, HBM],
        scratch_shapes=[pltpu.SemaphoreType.DMA((2,))],
        compiler_params=params(4),
        cost_estimate=cheap(),
        name="stage",
    )(w, x)


def pick_kernel(place, own_ref, *refs):
    chip = place[2]
    out_ref = refs[-1]
    value = own_ref[...]
    for d, value_ref in zip(ROUND[1:], refs):
        value = jnp.where(chip == d, value_ref[...], value)
    out_ref[...] = value


def pick(place, own, received, after):
    return pl.pallas_call(
        pick_kernel,
        out_shape=jax.ShapeDtypeStruct(own.shape, own.dtype),
        in_specs=[SMEM] + [VMEM] * CHIPS + [HBM] * len(after),
        out_specs=VMEM,
        compiler_params=params(4),
        cost_estimate=cheap(),
        name="pick",
    )(place, own, *received, *after)


def qkv_kernel(layered, *refs):
    refs = list(refs)
    place, x_ref = refs.pop(0), refs.pop(0)
    pieces = [refs.pop(0) for _ in range(2 * CHIPS)] if layered else []
    even_ref, odd_ref, w_ref = refs.pop(0), refs.pop(0), refs.pop(0)
    base_ref = refs.pop(0) if layered else None
    out_ref, lhs = refs
    core, chip, layer = place[1], place[2], place[3]
    rows, columns = x_ref.shape
    width = w_ref.shape[2]

    if layered:
        size = rows // (2 * CHIPS)
        for number, piece in enumerate(pieces):
            half = core if number < CHIPS else 1 - core
            quarter = jnp.bitwise_xor(chip, ROUND[number % CHIPS] ^ (CHIPS - 1))
            start = (half * CHIPS + quarter) * size
            place_rows = pl.ds(pl.multiple_of(start, size), size)
            tokens = x_ref[place_rows, :].astype(F32)
            added = tokens + piece[...].astype(F32)
            base_ref[place_rows, :] = jnp.where(layer == 1, added, tokens).astype(BF16)
    @pl.when(layer == (1 if layered else 0))
    def _():
        vectors = jnp.where(core == 0, even_ref[...], odd_ref[...])
        gain, bias = vectors[0:1, :], vectors[1:2, :]
        row16 = lax.broadcasted_iota(jnp.int32, (EXTRA, columns), 0)
        tail = jnp.zeros((EXTRA, columns), F32)
        for number, vector in enumerate(split_parts(gain, 2) + split_parts(bias, 2)):
            tail = tail + jnp.where(row16 == number, vector, 0.0)
        lhs[rows : rows + EXTRA, :] = tail.astype(BF16)

        source = base_ref if layered else x_ref
        firsts, seconds = [], []
        for start, size in segments_of(rows):
            value = source[start : start + size, :].astype(F32)
            first = jnp.sum(value, axis=1, keepdims=True)
            second = jnp.sum(value * value, axis=1, keepdims=True)
            lhs[start : start + size, :] = ((value - first * (1.0 / columns)) * gain).astype(BF16)
            lane = lax.broadcasted_iota(jnp.int32, (size, 128), 1)
            turned = jnp.where(lane == 0, first, jnp.where(lane == 1, second, 0.0)).T
            firsts.append(turned[0:1, :])
            seconds.append(turned[1:2, :])
        blank = jnp.zeros((1, width), F32)
        joined = lambda lines: jnp.concatenate(lines, axis=1) if len(lines) > 1 else lines[0]
        lines = ending(blank, blank, joined(firsts), joined(seconds), width)
        out_row = lax.broadcasted_iota(jnp.int32, (EXTRA, width), 0)

        for pair in range(TP // 2):
            weights = jnp.concatenate([w_ref[2 * pair], w_ref[2 * pair + 1]], axis=1)
            result = jnp.dot(lhs[...], weights, preferred_element_type=F32)
            for side in range(2):
                head = 2 * pair + side
                part = result[:, side * width : (side + 1) * width]
                ends = part[rows : rows + EXTRA, :]
                table = lines
                vectors = split_parts(ends[0:1] + ends[1:2], 2) + split_parts(ends[2:3] + ends[3:4], 2)
                for number, vector in enumerate(vectors):
                    table = table + jnp.where(out_row == number, vector, 0.0)
                out_ref[head, 0:rows, :] = part[0:rows, :].astype(BF16)
                out_ref[head, rows : rows + EXTRA, :] = table.astype(BF16)


def qkv(place, x, pieces, even, odd, w):
    rows, columns = x.shape
    heads, _, width = w.shape
    shapes = [jax.ShapeDtypeStruct((heads, rows + EXTRA, width), BF16)]
    if pieces:
        shapes = [jax.ShapeDtypeStruct((rows, columns), BF16)] + shapes
    out = pl.pallas_call(
        functools.partial(qkv_kernel, bool(pieces)),
        out_shape=shapes,
        in_specs=[SMEM] + [VMEM] * (len(pieces) + 4),
        out_specs=[VMEM] * len(shapes),
        scratch_shapes=[pltpu.VMEM((rows + EXTRA, columns), BF16)],
        compiler_params=params(24),
        cost_estimate=cheap(),
        name="qkv",
    )(place, x, *pieces, even, odd, w)
    return out if pieces else (None, out[0])


def attention_kernel(features, phase, place, pieces_ref, out_ref):
    rows, head_dim = out_ref.shape

    @pl.when(place[3] == phase)
    def _():
        total, scale, offset = combine([pieces_ref.at[t] for t in range(TP)], features // TP)
        joined = (total * scale + offset).astype(BF16)
        query = joined[:, :head_dim]
        key = joined[:, head_dim : 2 * head_dim]
        value = joined[:, 2 * head_dim :]
        scores = lax.dot_general(
            query, key, (((1,), (1,)), ((), ())), preferred_element_type=F32
        ) * (1.0 / head_dim**0.5)
        at_query = lax.broadcasted_iota(jnp.int32, (rows, rows), 0)
        at_key = lax.broadcasted_iota(jnp.int32, (rows, rows), 1)
        scores = jnp.where(at_key <= at_query, scores, -1e30)
        highest = jnp.max(scores, axis=1, keepdims=True)
        lifted = jnp.exp(scores - highest)
        weights = (lifted * (1.0 / jnp.sum(lifted, axis=1, keepdims=True))).astype(BF16)
        out_ref[...] = jnp.dot(weights, value, preferred_element_type=F32).astype(BF16)


def attention(place, pieces, features, phase):
    rows = pieces.shape[1] - EXTRA
    head_dim = pieces.shape[2] // 3
    return pl.pallas_call(
        functools.partial(attention_kernel, features, phase),
        out_shape=jax.ShapeDtypeStruct((rows, head_dim), BF16),
        in_specs=[SMEM, VMEM],
        out_specs=VMEM,
        compiler_params=params(24),
        cost_estimate=cheap(),
        name="attention",
    )(place, pieces)


def project_kernel(keeping, passing, place, *refs):
    refs = list(refs)
    pieces = [refs.pop(0) for _ in range(TP)]
    w_ref = refs.pop(0)
    old_ref = refs.pop(0) if passing else None
    out_ref, side = refs
    me, core, layer = place[0], place[1], place[3]
    rows, head_dim = out_ref.shape[0], pieces[0].shape[1]

    @pl.when(layer == (1 if passing else 0))
    def _():
        half = core if keeping else 1 - core
        inside = pl.ds(pl.multiple_of(half * rows, rows), rows)
        for d, piece in zip(AWAY, pieces):
            start = pl.multiple_of(jnp.bitwise_xor(me, d) * head_dim, head_dim)
            side[:, pl.ds(start, head_dim)] = piece[inside, :]
        out_ref[...] = jnp.dot(side[...], w_ref[...], preferred_element_type=F32).astype(BF16)

    if passing:

        @pl.when(layer == 0)
        def _():
            out_ref[...] = old_ref[...]


def project(keeping, place, pieces, w, old):
    rows, head_dim = pieces[0].shape
    columns = w.shape[1]
    return pl.pallas_call(
        functools.partial(project_kernel, keeping, bool(old)),
        out_shape=jax.ShapeDtypeStruct((rows // 2, columns), BF16),
        in_specs=[SMEM] + [VMEM] * (TP + 1 + len(old)),
        out_specs=VMEM,
        scratch_shapes=[pltpu.VMEM((rows // 2, TP * head_dim), BF16)],
        compiler_params=params(16),
        cost_estimate=cheap(),
        name="project",
    )(place, *pieces, w, *old)


def quarters_kernel(place, keep_ref, got_ref, *outs):
    chip = place[2]
    size = outs[0].shape[0]
    for d, out_ref in zip(ROUND, outs):
        rows = pl.ds(pl.multiple_of(jnp.bitwise_xor(chip, d) * size, size), size)
        out_ref[...] = (keep_ref[rows, :].astype(F32) + got_ref[rows, :].astype(F32)).astype(BF16)


def quarters(place, keep, got):
    rows, columns = keep.shape
    return pl.pallas_call(
        quarters_kernel,
        out_shape=[jax.ShapeDtypeStruct((rows // CHIPS, columns), BF16)] * CHIPS,
        in_specs=[SMEM, VMEM, VMEM],
        out_specs=[VMEM] * CHIPS,
        compiler_params=params(16),
        cost_estimate=cheap(),
        name="quarters",
    )(place, keep, got)


def finish_kernel(place, base_ref, keep_ref, got_ref, send_ref, other_keep_ref, *refs):
    own, others, out_ref = refs[:CHIPS], refs[CHIPS : 2 * CHIPS], refs[2 * CHIPS]
    core, chip = place[1], place[2]
    half_rows = keep_ref.shape[0]
    size = half_rows // CHIPS
    second = core.astype(F32)
    for half, sums, mine, theirs in (
        (core, own, keep_ref, got_ref),
        (1 - core, others, send_ref, other_keep_ref),
    ):
        for slot, d in enumerate(ROUND):
            start = pl.multiple_of(jnp.bitwise_xor(chip, d) * size, size)
            inside = pl.ds(start, size)
            whole = pl.ds(pl.multiple_of(half * half_rows + start, size), size)
            out_ref[whole, :] = (
                base_ref[whole, :].astype(F32)
                + sums[slot][...].astype(F32)
                + mine[inside, :].astype(F32)
                + second * theirs[inside, :].astype(F32)
            ).astype(BF16)


def finish(place, base, keep, got, send, other_keep, own, others):
    return pl.pallas_call(
        finish_kernel,
        out_shape=jax.ShapeDtypeStruct(base.shape, BF16),
        in_specs=[SMEM] + [VMEM] * (5 + 2 * CHIPS),
        out_specs=VMEM,
        compiler_params=params(24),
        cost_estimate=cheap(),
        name="finish",
    )(place, base, keep, got, send, other_keep, *own, *others)


def over_tp(value):
    return lax.all_to_all(value, "tp", 0, 0, tiled=True)


def over_cores(value):
    return lax.ppermute(value, "section", [(s, s ^ 1) for s in range(2 * SPAN)])


def over_chips(value, d):
    return lax.ppermute(value, "section", [(s, s ^ (2 * d)) for s in range(2 * SPAN)])


def spread(value):
    return [
        lax.ppermute(value, "tp", [(t, t ^ d) for t in range(TP)]) if d else value for d in AWAY
    ]


def over_layer(values):
    return [over_chips(value, d) if d else value for d, value in zip(ROUND, values)]


def on_device(tokens, ln_gain, ln_bias, w_qkv, w_out):
    section = lax.axis_index("section")
    me = lax.axis_index("tp")
    core = section % 2
    chip = (section // 2) % CHIPS
    layer = section // SPAN
    place = jnp.stack([me, core, chip, layer]).astype(jnp.int32)
    weight_in = w_qkv[0]
    weight_back = w_out[0]
    features = tokens.shape[1] * TP

    vectors = jnp.concatenate([ln_gain, ln_bias], axis=0)
    weight_in, tokens = stage(weight_in, tokens)
    received = [over_chips(vectors, d) for d in ROUND[1:]]
    even = pick(place, vectors, received, [weight_in])
    odd = over_cores(even)

    _, part = qkv(place, tokens, [], even, odd, weight_in)
    out = attention(place, over_tp(part), features, 0)
    heads = spread(out)
    send = project(False, place, heads, weight_back, [])
    got = over_cores(send)
    keep = project(True, place, heads, weight_back, [])
    arrived = over_layer(quarters(place, keep, got))
    total = sum(value.astype(F32) for value in arrived).astype(BF16)
    own = over_layer([over_chips(total, 2 * CHIPS - 1)] * CHIPS)
    others = [over_cores(value) for value in own]

    base, part = qkv(place, tokens, own + others, even, odd, weight_in)
    out = attention(place, over_tp(part), features, 1)
    heads = spread(out)
    send = project(False, place, heads, weight_back, [send])
    got = over_cores(send)
    keep = project(True, place, heads, weight_back, [keep])
    other_keep = over_cores(keep)
    arrived = over_layer(quarters(place, keep, got))
    before = []
    for d in ROUND:
        target = jnp.bitwise_xor(chip, d)
        before.append(
            sum(
                jnp.where(jnp.bitwise_xor(chip, e) < target, value.astype(F32), 0.0)
                for e, value in zip(ROUND, arrived)
            ).astype(BF16)
        )
    own = over_layer(before)
    others = [over_cores(value) for value in own]
    return finish(place, base, keep, got, send, other_keep, own, others)[None]


def solution(mesh):
    return jax.shard_map(
        on_device,
        mesh=mesh,
        in_specs=(
            P("dp", "tp"),
            P("section", "tp"),
            P("section", "tp"),
            P("section", None, "tp", None),
            P("section", None, "tp"),
        ),
        out_specs=P("section", "dp", "tp"),
        check_vma=False,
    )
```

```python
import functools

import jax
import jax.numpy as jnp
from jax import lax
from jax.experimental import pallas as pl
from jax.experimental.pallas import tpu as pltpu
from jax.sharding import PartitionSpec as P

SPAN = 8
TP = 8
CHIPS = 4
EXTRA = 16
EPS = 1e-05
ROUND = (0, 2, 3, 1)
AWAY = (0, 5, 7, 3, 1, 4, 6, 2)
SEGMENT = 256
BF16 = jnp.bfloat16
F32 = jnp.float32
VMEM = pl.BlockSpec(memory_space=pltpu.VMEM)
SMEM = pl.BlockSpec(memory_space=pltpu.SMEM)
HBM = pl.BlockSpec(memory_space=pl.ANY)


def params(mib):
    return pltpu.CompilerParams(vmem_limit_bytes=mib * 1024 * 1024)


def segments_of(rows):
    size = min(rows, SEGMENT)
    return [(start, size) for start in range(0, rows, size)]


def split_parts(value, count):
    parts = []
    for _ in range(count):
        part = value.astype(BF16).astype(F32)
        parts.append(part)
        value = value - part
    return parts


def ending(head_line, offset_line, first, second, width):
    vectors = split_parts(head_line, 2) + split_parts(offset_line, 2)
    for line in (first, second):
        for start, size in segments_of(line.shape[1]):
            for part in split_parts(line[:, start : start + size], 3):
                vectors.append(jnp.concatenate([part, jnp.zeros((1, width - size), F32)], axis=1))
    row = lax.broadcasted_iota(jnp.int32, (EXTRA, width), 0)
    table = jnp.zeros((EXTRA, width), F32)
    for number, vector in enumerate(vectors):
        table = table + jnp.where(row == number, vector, 0.0)
    return table


def combine(pieces, features):
    rows, width = pieces[0].shape[0] - EXTRA, pieces[0].shape[1]
    segments = segments_of(rows)
    total = jnp.zeros((rows, width), F32)
    heads, firsts, offset, second = [], [], 0.0, 0.0
    for piece in pieces:
        total = total + piece[0:rows, :].astype(F32)
        ends = piece[rows : rows + EXTRA, :].astype(F32)
        heads.append(ends[0:1] + ends[1:2])
        offset = offset + (ends[2:3] + ends[3:4])
        lines = []
        for kind in range(2):
            spans = []
            for number, (_, size) in enumerate(segments):
                slot = 4 + (kind * len(segments) + number) * 3
                spans.append((ends[slot : slot + 1] + ends[slot + 1 : slot + 2] + ends[slot + 2 : slot + 3])[:, :size])
            lines.append(jnp.concatenate(spans, axis=1) if len(spans) > 1 else spans[0])
        firsts.append(lines[0])
        second = second + lines[1]
    first = sum(firsts)
    count = features * len(pieces)
    average = first * (1.0 / count)
    variance = second * (1.0 / count) - average * average
    scale = lax.rsqrt(jnp.maximum(variance, 0.0) + EPS)
    line_row = lax.broadcasted_iota(jnp.int32, (128, rows), 0)
    table = jnp.where(line_row == TP, scale, 0.0)
    head_row = lax.broadcasted_iota(jnp.int32, (128, width), 0)
    matrix = jnp.zeros((128, width), F32)
    for number in range(len(pieces)):
        table = jnp.where(line_row == number, firsts[number] * (1.0 / features) - average, table)
        matrix = jnp.where(head_row == number, heads[number], matrix)
    turned = table.T
    total = total + jnp.dot(
        turned, matrix, preferred_element_type=F32, precision=lax.Precision.HIGHEST
    )
    return total, turned[:, TP : TP + 1], offset


def cheap():
    return pl.CostEstimate(flops=1, bytes_accessed=1, transcendentals=0)


def stage_kernel(value_ref, *refs):
    out_ref, sem = refs[-2:]
    copy = pltpu.make_async_copy(value_ref, out_ref, sem)
    copy.start()
    copy.wait()


def stage(value, after):
    return pl.pallas_call(
        stage_kernel,
        out_shape=jax.ShapeDtypeStruct(value.shape, value.dtype),
        in_specs=[HBM] * (1 + len(after)),
        out_specs=HBM,
        scratch_shapes=[pltpu.SemaphoreType.DMA],
        compiler_params=params(4),
        cost_estimate=cheap(),
        name="stage",
    )(value, *after)


def pick_kernel(place, own_ref, *refs):
    chip = place[2]
    out_ref = refs[-1]
    value = own_ref[...]
    for d, value_ref in zip(ROUND[1:], refs):
        value = jnp.where(chip == d, value_ref[...], value)
    out_ref[...] = value


def pick(place, own, received, after):
    return pl.pallas_call(
        pick_kernel,
        out_shape=jax.ShapeDtypeStruct(own.shape, own.dtype),
        in_specs=[SMEM] + [VMEM] * CHIPS + [HBM] * len(after),
        out_specs=VMEM,
        compiler_params=params(4),
        cost_estimate=cheap(),
        name="pick",
    )(place, own, *received, *after)


def qkv_kernel(layered, *refs):
    refs = list(refs)
    place, x_ref = refs.pop(0), refs.pop(0)
    pieces = [refs.pop(0) for _ in range(2 * CHIPS)] if layered else []
    even_ref, odd_ref, w_ref = refs.pop(0), refs.pop(0), refs.pop(0)
    base_ref = refs.pop(0) if layered else None
    out_ref, lhs = refs
    core, chip, layer = place[1], place[2], place[3]
    rows, columns = x_ref.shape
    width = w_ref.shape[2]

    if layered:
        size = rows // (2 * CHIPS)
        for number, piece in enumerate(pieces):
            half = core if number < CHIPS else 1 - core
            quarter = jnp.bitwise_xor(chip, ROUND[number % CHIPS] ^ (CHIPS - 1))
            start = (half * CHIPS + quarter) * size
            place_rows = pl.ds(pl.multiple_of(start, size), size)
            tokens = x_ref[place_rows, :].astype(F32)
            added = tokens + piece[...].astype(F32)
            base_ref[place_rows, :] = jnp.where(layer == 1, added, tokens).astype(BF16)
    @pl.when(layer == (1 if layered else 0))
    def _():
        vectors = jnp.where(core == 0, even_ref[...], odd_ref[...])
        gain, bias = vectors[0:1, :], vectors[1:2, :]
        row16 = lax.broadcasted_iota(jnp.int32, (EXTRA, columns), 0)
        tail = jnp.zeros((EXTRA, columns), F32)
        for number, vector in enumerate(split_parts(gain, 2) + split_parts(bias, 2)):
            tail = tail + jnp.where(row16 == number, vector, 0.0)
        lhs[rows : rows + EXTRA, :] = tail.astype(BF16)

        source = base_ref if layered else x_ref
        firsts, seconds = [], []
        for start, size in segments_of(rows):
            value = source[start : start + size, :].astype(F32)
            first = jnp.sum(value, axis=1, keepdims=True)
            second = jnp.sum(value * value, axis=1, keepdims=True)
            lhs[start : start + size, :] = ((value - first * (1.0 / columns)) * gain).astype(BF16)
            lane = lax.broadcasted_iota(jnp.int32, (size, 128), 1)
            turned = jnp.where(lane == 0, first, jnp.where(lane == 1, second, 0.0)).T
            firsts.append(turned[0:1, :])
            seconds.append(turned[1:2, :])
        blank = jnp.zeros((1, width), F32)
        joined = lambda lines: jnp.concatenate(lines, axis=1) if len(lines) > 1 else lines[0]
        lines = ending(blank, blank, joined(firsts), joined(seconds), width)
        out_row = lax.broadcasted_iota(jnp.int32, (EXTRA, width), 0)

        for pair in range(TP // 2):
            weights = jnp.concatenate([w_ref[2 * pair], w_ref[2 * pair + 1]], axis=1)
            result = jnp.dot(lhs[...], weights, preferred_element_type=F32)
            for side in range(2):
                head = 2 * pair + side
                part = result[:, side * width : (side + 1) * width]
                ends = part[rows : rows + EXTRA, :]
                table = lines
                vectors = split_parts(ends[0:1] + ends[1:2], 2) + split_parts(ends[2:3] + ends[3:4], 2)
                for number, vector in enumerate(vectors):
                    table = table + jnp.where(out_row == number, vector, 0.0)
                out_ref[head, 0:rows, :] = part[0:rows, :].astype(BF16)
                out_ref[head, rows : rows + EXTRA, :] = table.astype(BF16)


def qkv(place, x, pieces, even, odd, w):
    rows, columns = x.shape
    heads, _, width = w.shape
    shapes = [jax.ShapeDtypeStruct((heads, rows + EXTRA, width), BF16)]
    if pieces:
        shapes = [jax.ShapeDtypeStruct((rows, columns), BF16)] + shapes
    out = pl.pallas_call(
        functools.partial(qkv_kernel, bool(pieces)),
        out_shape=shapes,
        in_specs=[SMEM] + [VMEM] * (len(pieces) + 4),
        out_specs=[VMEM] * len(shapes),
        scratch_shapes=[pltpu.VMEM((rows + EXTRA, columns), BF16)],
        compiler_params=params(24),
        cost_estimate=cheap(),
        name="qkv",
    )(place, x, *pieces, even, odd, w)
    return out if pieces else (None, out[0])


def attention_kernel(features, phase, place, pieces_ref, out_ref):
    rows, head_dim = out_ref.shape

    @pl.when(place[3] == phase)
    def _():
        total, scale, offset = combine([pieces_ref.at[t] for t in range(TP)], features // TP)
        joined = (total * scale + offset).astype(BF16)
        query = joined[:, :head_dim]
        key = joined[:, head_dim : 2 * head_dim]
        value = joined[:, 2 * head_dim :]
        scores = lax.dot_general(
            query, key, (((1,), (1,)), ((), ())), preferred_element_type=F32
        ) * (1.0 / head_dim**0.5)
        at_query = lax.broadcasted_iota(jnp.int32, (rows, rows), 0)
        at_key = lax.broadcasted_iota(jnp.int32, (rows, rows), 1)
        scores = jnp.where(at_key <= at_query, scores, -1e30)
        highest = jnp.max(scores, axis=1, keepdims=True)
        lifted = jnp.exp(scores - highest)
        weights = (lifted * (1.0 / jnp.sum(lifted, axis=1, keepdims=True))).astype(BF16)
        out_ref[...] = jnp.dot(weights, value, preferred_element_type=F32).astype(BF16)


def attention(place, pieces, features, phase):
    rows = pieces.shape[1] - EXTRA
    head_dim = pieces.shape[2] // 3
    return pl.pallas_call(
        functools.partial(attention_kernel, features, phase),
        out_shape=jax.ShapeDtypeStruct((rows, head_dim), BF16),
        in_specs=[SMEM, VMEM],
        out_specs=VMEM,
        compiler_params=params(24),
        cost_estimate=cheap(),
        name="attention",
    )(place, pieces)


def project_kernel(keeping, passing, place, *refs):
    refs = list(refs)
    pieces = [refs.pop(0) for _ in range(TP)]
    w_ref = refs.pop(0)
    old_ref = refs.pop(0) if passing else None
    out_ref, side = refs
    me, core, layer = place[0], place[1], place[3]
    rows, head_dim = out_ref.shape[0], pieces[0].shape[1]

    @pl.when(layer == (1 if passing else 0))
    def _():
        half = core if keeping else 1 - core
        inside = pl.ds(pl.multiple_of(half * rows, rows), rows)
        for d, piece in zip(AWAY, pieces):
            start = pl.multiple_of(jnp.bitwise_xor(me, d) * head_dim, head_dim)
            side[:, pl.ds(start, head_dim)] = piece[inside, :]
        out_ref[...] = jnp.dot(side[...], w_ref[...], preferred_element_type=F32).astype(BF16)

    if passing:

        @pl.when(layer == 0)
        def _():
            out_ref[...] = old_ref[...]


def project(keeping, place, pieces, w, old):
    rows, head_dim = pieces[0].shape
    columns = w.shape[1]
    return pl.pallas_call(
        functools.partial(project_kernel, keeping, bool(old)),
        out_shape=jax.ShapeDtypeStruct((rows // 2, columns), BF16),
        in_specs=[SMEM] + [VMEM] * (TP + 1 + len(old)),
        out_specs=VMEM,
        scratch_shapes=[pltpu.VMEM((rows // 2, TP * head_dim), BF16)],
        compiler_params=params(16),
        cost_estimate=cheap(),
        name="project",
    )(place, *pieces, w, *old)


def quarters_kernel(place, keep_ref, got_ref, *outs):
    chip = place[2]
    size = outs[0].shape[0]
    for d, out_ref in zip(ROUND, outs):
        rows = pl.ds(pl.multiple_of(jnp.bitwise_xor(chip, d) * size, size), size)
        out_ref[...] = (keep_ref[rows, :].astype(F32) + got_ref[rows, :].astype(F32)).astype(BF16)


def quarters(place, keep, got):
    rows, columns = keep.shape
    return pl.pallas_call(
        quarters_kernel,
        out_shape=[jax.ShapeDtypeStruct((rows // CHIPS, columns), BF16)] * CHIPS,
        in_specs=[SMEM, VMEM, VMEM],
        out_specs=[VMEM] * CHIPS,
        compiler_params=params(16),
        cost_estimate=cheap(),
        name="quarters",
    )(place, keep, got)


def finish_kernel(place, base_ref, keep_ref, got_ref, send_ref, other_keep_ref, *refs):
    own, others, out_ref = refs[:CHIPS], refs[CHIPS : 2 * CHIPS], refs[2 * CHIPS]
    core, chip = place[1], place[2]
    half_rows = keep_ref.shape[0]
    size = half_rows // CHIPS
    second = core.astype(F32)
    for half, sums, mine, theirs in (
        (core, own, keep_ref, got_ref),
        (1 - core, others, send_ref, other_keep_ref),
    ):
        for slot, d in enumerate(ROUND):
            start = pl.multiple_of(jnp.bitwise_xor(chip, d) * size, size)
            inside = pl.ds(start, size)
            whole = pl.ds(pl.multiple_of(half * half_rows + start, size), size)
            out_ref[whole, :] = (
                base_ref[whole, :].astype(F32)
                + sums[slot][...].astype(F32)
                + mine[inside, :].astype(F32)
                + second * theirs[inside, :].astype(F32)
            ).astype(BF16)


def finish(place, base, keep, got, send, other_keep, own, others):
    return pl.pallas_call(
        finish_kernel,
        out_shape=jax.ShapeDtypeStruct(base.shape, BF16),
        in_specs=[SMEM] + [VMEM] * (5 + 2 * CHIPS),
        out_specs=VMEM,
        compiler_params=params(24),
        cost_estimate=cheap(),
        name="finish",
    )(place, base, keep, got, send, other_keep, *own, *others)


def over_tp(value):
    return lax.all_to_all(value, "tp", 0, 0, tiled=True)


def over_cores(value):
    return lax.ppermute(value, "section", [(s, s ^ 1) for s in range(2 * SPAN)])


def over_chips(value, d):
    return lax.ppermute(value, "section", [(s, s ^ (2 * d)) for s in range(2 * SPAN)])


def spread(value):
    return [
        lax.ppermute(value, "tp", [(t, t ^ d) for t in range(TP)]) if d else value for d in AWAY
    ]


def over_layer(values):
    return [over_chips(value, d) if d else value for d, value in zip(ROUND, values)]


def on_device(tokens, ln_gain, ln_bias, w_qkv, w_out):
    section = lax.axis_index("section")
    me = lax.axis_index("tp")
    core = section % 2
    chip = (section // 2) % CHIPS
    layer = section // SPAN
    place = jnp.stack([me, core, chip, layer]).astype(jnp.int32)
    weight_in = w_qkv[0]
    weight_back = w_out[0]
    features = tokens.shape[1] * TP

    vectors = jnp.concatenate([ln_gain, ln_bias], axis=0)
    weight_in = stage(weight_in, [])
    received = [over_chips(vectors, d) for d in ROUND[1:]]
    even = pick(place, vectors, received, [weight_in])
    odd = over_cores(even)
    tokens = stage(tokens, [even])

    _, part = qkv(place, tokens, [], even, odd, weight_in)
    out = attention(place, over_tp(part), features, 0)
    heads = spread(out)
    send = project(False, place, heads, weight_back, [])
    got = over_cores(send)
    keep = project(True, place, heads, weight_back, [])
    arrived = over_layer(quarters(place, keep, got))
    total = sum(value.astype(F32) for value in arrived).astype(BF16)
    own = over_layer([over_chips(total, 2 * CHIPS - 1)] * CHIPS)
    others = [over_cores(value) for value in own]

    base, part = qkv(place, tokens, own + others, even, odd, weight_in)
    out = attention(place, over_tp(part), features, 1)
    heads = spread(out)
    send = project(False, place, heads, weight_back, [send])
    got = over_cores(send)
    keep = project(True, place, heads, weight_back, [keep])
    other_keep = over_cores(keep)
    arrived = over_layer(quarters(place, keep, got))
    before = []
    for d in ROUND:
        target = jnp.bitwise_xor(chip, d)
        before.append(
            sum(
                jnp.where(jnp.bitwise_xor(chip, e) < target, value.astype(F32), 0.0)
                for e, value in zip(ROUND, arrived)
            ).astype(BF16)
        )
    own = over_layer(before)
    others = [over_cores(value) for value in own]
    return finish(place, base, keep, got, send, other_keep, own, others)[None]


def solution(mesh):
    return jax.shard_map(
        on_device,
        mesh=mesh,
        in_specs=(
            P("dp", "tp"),
            P("section", "tp"),
            P("section", "tp"),
            P("section", None, "tp", None),
            P("section", None, "tp"),
        ),
        out_specs=P("section", "dp", "tp"),
        check_vma=False,
    )
```
